512 devices in a mesh: seq: 64 (over z, x), chan: 8 (over y, core).
Axes of the slice: x: 4, y: 4, z: 16, core: 2. Of those that a mesh axis runs over, the one named last changes fastest.
Arguments:
- input_gate: bfloat16 [16384, 4096], P('seq', 'chan'), may hold values from -6 to 6
- output_gate: bfloat16 [16384, 4096], P('seq', 'chan'), may hold values from -6 to 6
- values: bfloat16 [16384, 4096], P('seq', 'chan'), may hold values from -6 to 6
- residual: bfloat16 [16384, 4096], P('seq', 'chan'), may hold values from -32 to 32
- cotangent: bfloat16 [16384, 4096], P('seq', 'chan'), may hold values from -6 to 6
- filters: float32 [16384, 4096], P('seq', 'chan'), may hold values from -0.046875 to 0.046875
- norm_gain: bfloat16 [4096], P('chan'), may hold values from 0.5 to 1.5
- doc_spans: int32 [4, 2], replicated, may hold values from 0 to 16384, as said below
Outputs:
- normed: bfloat16 [16384, 4096], P('seq', 'chan')
- residual_grad: bfloat16 [16384, 4096], P('seq', 'chan')
- input_gate_grad: bfloat16 [16384, 4096], P('seq', 'chan')
- output_gate_grad: bfloat16 [16384, 4096], P('seq', 'chan')
- values_grad: bfloat16 [16384, 4096], P('seq', 'chan')
- filter_grad: float32 [16384, 4096], P('seq', 'chan')
The draws below stay inside these ranges and needn't reach their ends.
Inputs may be any that keep to these rules, and one draw needn't show every extreme that they name: `doc_spans`: row d holds the first token of document d and the token after its last; documents are in increasing order, disjoint, never empty, and begin and end at multiples of 512; the first begins at 0 and the last ends at 16384; a gap between two documents is at most 512 tokens and its tokens belong to no document.
All inputs are finite; a program needn't handle non-finite values.
Results may differ from the reference program's by a relative error of at most 0.0049.
Values may be sent and summed in bfloat16 or wider, within the bound.
No kernel may reach another device: no remote copies, remote signals or barrier semaphores. Data moves between devices by JAX's collectives and lax.ppermute only.
A program may use at most 64 MiB of HBM per device.

```python
import math
import jax
import jax.numpy as jnp
from jax import lax

D = 4096
BLOCK = 512
TAPS = 16384
DOCS = 4
TOKENS = 16384


def draw_residual(key, part):
    key = jax.random.fold_in(key, 5)
    first_key, second_key = jax.random.split(key)
    column_scale = 0.25 * 10.0 ** (jnp.arange(D, dtype=jnp.float32) / D)
    row_scale = 10.0 ** (jax.random.uniform(second_key, (TOKENS, 1), jnp.float32) - 0.5)
    noise = jnp.clip(jax.random.normal(first_key, (TOKENS, D), jnp.float32), -4.0, 4.0)
    return (noise * row_scale * column_scale[None, :]).astype(jnp.bfloat16)


def draw_doc_spans(key, part):
    key = jax.random.fold_in(key, 9)
    first_key, second_key, third_key = jax.random.split(key, 3)
    block_count = TOKENS // BLOCK
    short_most = max(1, block_count // (4 * DOCS))
    lengths = jax.random.randint(first_key, (DOCS,), 1, short_most + 1).astype(jnp.int32)
    long_place = jax.random.randint(third_key, (), 0, DOCS).astype(jnp.int32)
    is_long = jnp.arange(DOCS, dtype=jnp.int32) == long_place
    others = jnp.sum(jnp.where(is_long, 0, lengths)).astype(jnp.int32)
    lengths = jnp.where(is_long, block_count - others, lengths).astype(jnp.int32)
    bounds = jnp.cumsum(lengths).astype(jnp.int32)
    starts = (bounds - lengths).astype(jnp.int32)
    padding = jax.random.randint(second_key, (DOCS,), 0, 2).astype(jnp.int32)
    padding = padding * (lengths > 1).astype(jnp.int32)
    padding = padding.at[DOCS - 1].set(0)
    return (jnp.stack([starts, bounds - padding], axis=1) * BLOCK).astype(jnp.int32)


def block_scale(rng, dims, pieces, smallest, top_value):
    level = 1.0
    for dim, blocks in pieces:
        heights = jax.random.uniform(jax.random.fold_in(jax.random.fold_in(rng, 6), dim), (blocks,), jnp.float32, smallest / len(pieces), top_value / len(pieces))
        level = level * jnp.repeat(jnp.exp(heights), dims[dim] // blocks).reshape((-1,) + (1,) * (len(dims) - 1 - dim))
    return level


def bell_draw(key, dims, width, bound, shards=(), held_as=jnp.bfloat16):
    drawn = jax.random.normal(key, dims, jnp.float32) * width
    if len(shards) > 0:
        drawn = block_scale(key, dims, shards, -0.22, 0.18) * drawn
    return jnp.clip(drawn, min=-bound, max=bound).astype(held_as)


def setup_inputs(seed: int = 0) -> dict:
    key_list = jax.random.split(jax.random.key(seed), 9)
    input_gate = bell_draw(key_list[0], (TOKENS, D), 1.0, 6.0, ((0, 64), (1, 8)))
    output_gate = bell_draw(key_list[1], (TOKENS, D), 1.0, 6.0, ((0, 64), (1, 8)))
    values = bell_draw(key_list[2], (TOKENS, D), 1.0, 6.0, ((0, 64), (1, 8)))
    residual = draw_residual(jax.random.fold_in(key_list[8], 71), 0)
    cotangent = bell_draw(key_list[4], (TOKENS, D), 1.0, 6.0, ((0, 64), (1, 8)))
    filters = bell_draw(key_list[5], (TAPS, D), TAPS ** -0.5, 0.046875, ((0, 64), (1, 8)), jnp.float32)
    norm_gain = jnp.clip(1.0 + 0.1 * jax.random.normal(key_list[6], (D,), jnp.float32), 0.5, 1.5).astype(jnp.bfloat16)
    doc_spans = draw_doc_spans(jax.random.fold_in(key_list[8], 71), 0)
    return {"input_gate": input_gate, "output_gate": output_gate, "values": values, "residual": residual, "cotangent": cotangent, "filters": filters, "norm_gain": norm_gain, "doc_spans": doc_spans}


EPSILON = 1e-06

def doc_label(doc_spans, block_index):
    places = block_index * BLOCK
    inside = (doc_spans[:, 0] <= places[..., None]) & (places[..., None] < doc_spans[:, 1])
    labels = jnp.arange(1, doc_spans.shape[0] + 1, dtype=jnp.int32)
    return lax.optimization_barrier(jnp.sum(jnp.where(inside, labels, 0), axis=-1))

def reference(input_gate, output_gate, values, residual, cotangent, filters, norm_gain, doc_spans):
    used_taps = min(TAPS, TOKENS)
    block_count = TOKENS // BLOCK
    labels = doc_label(doc_spans, jnp.arange(block_count, dtype=jnp.int32))
    token_label = jnp.repeat(labels, BLOCK)
    doc_ids = jnp.arange(1, DOCS + 1, dtype=jnp.int32)
    masks = (token_label[None, :] == doc_ids[:, None]).astype(jnp.float32)
    length = TOKENS + used_taps
    group_width = math.gcd(D, 512)
    group_count = D // group_width

    def split_groups(array):
        return array.reshape(array.shape[0], group_count, group_width).transpose(1, 0, 2)

    def join_groups(array):
        return array.transpose(1, 0, 2).reshape(array.shape[1], D)

    def causal(gated_group, taps_group):
        filter_spec = jnp.fft.rfft(taps_group, n=length, axis=0)
        total = jnp.zeros_like(gated_group)
        for docnum in range(DOCS):
            weight = masks[docnum][:, None]
            spec = jnp.fft.rfft(gated_group * weight, n=length, axis=0)
            result = jnp.fft.irfft(spec * filter_spec, n=length, axis=0)[:TOKENS]
            total = total + weight * result
        return total

    def forward_group(paired):
        return causal(paired[0], paired[1])

    def backward_group(triple):
        unused, pull = jax.vjp(causal, triple[0], triple[1])
        return pull(triple[2])
    gated = (values.astype(jnp.float32) * input_gate.astype(jnp.float32)).astype(jnp.bfloat16)
    gated = lax.optimization_barrier(gated).astype(jnp.float32)
    taps = filters[:used_taps]
    conv = join_groups(lax.map(forward_group, (split_groups(gated), split_groups(taps))))
    gate_out = output_gate.astype(jnp.float32)
    mixed = residual.astype(jnp.float32) + conv * gate_out
    scale = lax.rsqrt(lax.optimization_barrier(jnp.sum(mixed * mixed, axis=1, keepdims=True)) / D + EPSILON)
    gain = norm_gain.astype(jnp.float32)[None, :]
    normed = (mixed * scale * gain).astype(jnp.bfloat16)
    lifted = cotangent.astype(jnp.float32) * gain
    inner = lax.optimization_barrier(jnp.sum(lifted * mixed, axis=1, keepdims=True)) / D
    mixed_grad = scale * (lifted - mixed * scale * scale * inner)
    conv_grad = (mixed_grad * gate_out).astype(jnp.bfloat16)
    conv_grad = lax.optimization_barrier(conv_grad).astype(jnp.float32)
    source_grad, tap_grad = lax.map(backward_group, (split_groups(gated), split_groups(taps), split_groups(conv_grad)))
    source_grad = join_groups(source_grad)
    filter_grad = join_groups(tap_grad) * TOKENS ** (-0.5)
    return (normed, mixed_grad.astype(jnp.bfloat16), (source_grad * values.astype(jnp.float32)).astype(jnp.bfloat16), (mixed_grad * conv).astype(jnp.bfloat16), (source_grad * input_gate.astype(jnp.float32)).astype(jnp.bfloat16), filter_grad)
```

```python
import functools

import jax
import jax.numpy as jnp
import ml_dtypes
import numpy as np
from jax import lax
from jax.experimental import pallas as pl
from jax.experimental.pallas import tpu as pltpu
from jax.sharding import PartitionSpec as P

D = 4096
BLOCK = 512
TOKENS = 16384
DOCS = 4
EPSILON = 1e-06
BLOCKS = TOKENS // BLOCK
FREQS = BLOCK
SPEC = 2 * FREQS
TILE = 4
PAD = TILE
ROWS = BLOCKS + PAD * (DOCS + 2)
F32 = jnp.float32
BF16 = jnp.bfloat16
VMEM_LIMIT = 56 * 1024 * 1024


def split_bf16(array):
    high = array.astype(ml_dtypes.bfloat16)
    low = (array - high.astype(np.float64)).astype(ml_dtypes.bfloat16)
    return np.stack([high, low])


def window_tables():
    places = np.arange(BLOCK, dtype=np.int64)
    odd = 2 * np.arange(FREQS, dtype=np.int64) + 1
    phase = (places[:, None] * odd[None, :] % (4 * BLOCK)) * (np.pi / (2 * BLOCK))
    forward = np.concatenate([np.cos(phase), -np.sin(phase)], axis=1)
    return split_bf16(forward), split_bf16(np.ascontiguousarray(forward.T))


def half_signs():
    lanes = lax.broadcasted_iota(jnp.int32, (1, 1, FREQS), 2)
    return (1 - 2 * (lanes % 2)).astype(F32)


def block_rows(slabs):
    count, chans, width = slabs.shape
    pairs = slabs.reshape(count // 2, 2, chans, width)
    joined = jnp.concatenate([pairs[:, 0], pairs[:, 1]], axis=2)
    return joined.reshape(count // 2 * chans, 2 * width)


def sender_slabs(rows, chans):
    width = rows.shape[1] // 2
    blocks = rows.reshape(rows.shape[0] // chans, 1, chans, 2 * width)
    joined = jnp.concatenate([blocks[..., :width], blocks[..., width:]], axis=1)
    return joined.reshape(2 * blocks.shape[0], chans, width)


def to_spectrum(rows, table_ref):
    rows = rows.astype(BF16)
    high = jnp.dot(rows, table_ref[0], preferred_element_type=F32)
    return high + jnp.dot(rows, table_ref[1], preferred_element_type=F32)


def from_spectrum(spec, table_ref):
    high = spec.astype(BF16)
    low = (spec - high.astype(F32)).astype(BF16)
    total = jnp.dot(high, table_ref[0], preferred_element_type=F32)
    total += jnp.dot(low, table_ref[0], preferred_element_type=F32)
    return total + jnp.dot(high, table_ref[1], preferred_element_type=F32)


def doc_bounds(spans_ref, doc):
    return spans_ref[2 * doc] // BLOCK, spans_ref[2 * doc + 1] // BLOCK


def columns():
    for lane in range(0, FREQS, 128):
        yield slice(lane, lane + 128), slice(FREQS + lane, FREQS + lane + 128)


def zero_sums():
    return [jnp.zeros((8, 128), F32) for _ in range(2 * TILE * (FREQS // 128))]


def store_tile(ref, row, sums):
    place = 0
    for re_lanes, im_lanes in columns():
        for i in range(TILE):
            ref[row + i, :, re_lanes] = sums[place]
            ref[row + i, :, im_lanes] = sums[place + 1]
            place += 2


def gate_kernel(values_ref, gate_ref, filters_ref, out_ref):
    gated = values_ref[...].astype(F32) * gate_ref[...].astype(F32)
    chans = out_ref.shape[1] // 2
    shape = (out_ref.shape[0], chans, out_ref.shape[2])
    both = jnp.concatenate(
        [gated.T.reshape(shape), filters_ref[...].T.reshape(shape)], axis=1
    )
    out_ref[...] = both.astype(BF16)


def forward_kernel(spans_ref, slabs_ref, table_ref, inverse_ref, conv_ref, source_ref, taps_ref, spec_ref):
    slabs = slabs_ref[...].astype(F32)
    signs = half_signs()
    source = to_spectrum(block_rows(slabs[:, :8]), table_ref).reshape(BLOCKS, 8, SPEC)
    spec_ref[pl.ds(0, BLOCKS)] = source
    taps = to_spectrum(block_rows(slabs[:, 8:]), table_ref).reshape(BLOCKS, 8, SPEC)
    real, imag = taps[..., :FREQS], taps[..., FREQS:]
    nothing = jnp.zeros((1, 8, FREQS), F32)
    before_real = jnp.concatenate([nothing, real[:-1]], axis=0)
    before_imag = jnp.concatenate([nothing, imag[:-1]], axis=0)
    taps_ref[pl.ds(0, PAD)] = jnp.zeros((PAD, 8, SPEC), F32)
    taps_ref[pl.ds(PAD, BLOCKS), :, :FREQS] = real - signs * before_imag
    taps_ref[pl.ds(PAD, BLOCKS), :, FREQS:] = imag + signs * before_real
    source_ref[...] = jnp.zeros((ROWS, 8, SPEC), F32)
    for doc in range(DOCS):
        start, end = doc_bounds(spans_ref, doc)

        @pl.loop(start, end)
        def _(n):
            source_ref[n + PAD * (doc + 1)] = spec_ref[n]

    spec_ref[...] = jnp.zeros(spec_ref.shape, F32)
    for doc in reversed(range(DOCS)):
        start, end = doc_bounds(spans_ref, doc)
        shift = PAD * (doc + 1)

        @pl.loop(0, (end - start + TILE - 1) // TILE)
        def _(tile):
            first = end - TILE * (tile + 1)

            def step(s, sums):
                sums = list(sums)
                place = 0
                for re_lanes, im_lanes in columns():
                    z_re = source_ref[s + shift, :, re_lanes]
                    z_im = source_ref[s + shift, :, im_lanes]
                    for i in range(TILE):
                        g_re = taps_ref[first + i - s + PAD, :, re_lanes]
                        g_im = taps_ref[first + i - s + PAD, :, im_lanes]
                        sums[place] += g_re * z_re - g_im * z_im
                        sums[place + 1] += g_re * z_im + g_im * z_re
                        place += 2
                return tuple(sums)

            sums = lax.fori_loop(start, first + TILE, step, tuple(zero_sums()))
            store_tile(spec_ref, first + PAD, sums)

    total = spec_ref[pl.ds(PAD, BLOCKS)].reshape(BLOCKS * 8, SPEC)
    conv = from_spectrum(total, inverse_ref) * (1.0 / BLOCK)
    conv_ref[...] = sender_slabs(conv, 8).astype(BF16)


def mixed_kernel(conv_ref, residual_ref, gate_ref, cotangent_ref, gain_ref, mixed_ref, token_conv_ref, sums_ref):
    tokens, width = residual_ref.shape
    conv = conv_ref[...].astype(F32).reshape(width, tokens).T
    mixed = residual_ref[...].astype(F32) + conv * gate_ref[...].astype(F32)
    lifted = cotangent_ref[...].astype(F32) * gain_ref[...].astype(F32)
    mixed_ref[...] = mixed
    token_conv_ref[...] = conv.astype(BF16)
    power = jnp.sum(mixed * mixed, axis=1, keepdims=True)
    inner = jnp.sum(lifted * mixed, axis=1, keepdims=True)
    lanes = lax.broadcasted_iota(jnp.int32, (tokens, 128), 1)
    both = jnp.where(lanes == 0, power, jnp.where(lanes == 1, inner, 0.0)).T[:8]
    sums_ref[...] = jnp.broadcast_to(both[None], sums_ref.shape)


def token_scales(sums_ref):
    total = jnp.sum(sums_ref[...], axis=0)
    padded = jnp.concatenate([total, jnp.zeros((120, total.shape[1]), F32)], axis=0).T
    scale = lax.rsqrt(padded[:, 0:1] / D + EPSILON)
    return scale, padded[:, 1:2] / D


def grad_kernel(sums_ref, mixed_ref, gate_ref, cotangent_ref, gain_ref, grad_ref):
    scale, inner = token_scales(sums_ref)
    lifted = cotangent_ref[...].astype(F32) * gain_ref[...].astype(F32)
    mixed_grad = scale * (lifted - mixed_ref[...] * (scale * scale * inner))
    conv_grad = mixed_grad * gate_ref[...].astype(F32)
    grad_ref[...] = conv_grad.T.reshape(grad_ref.shape).astype(BF16)


def token_kernel(sums_ref, mixed_ref, token_conv_ref, cotangent_ref, gain_ref, normed_ref, residual_grad_ref, gate_grad_ref):
    scale, inner = token_scales(sums_ref)
    gain = gain_ref[...].astype(F32)
    mixed = mixed_ref[...]
    lifted = cotangent_ref[...].astype(F32) * gain
    normed_ref[...] = (mixed * scale * gain).astype(BF16)
    mixed_grad = scale * (lifted - mixed * (scale * scale * inner))
    residual_grad_ref[...] = mixed_grad.astype(BF16)
    gate_grad_ref[...] = (mixed_grad * token_conv_ref[...].astype(F32)).astype(BF16)


def backward_kernel(spans_ref, slabs_ref, source_ref, taps_ref, table_ref, inverse_ref, out_ref, up_ref, spec_ref, lag_ref):
    signs = half_signs()
    up = to_spectrum(block_rows(slabs_ref[...].astype(F32)), table_ref)
    up_ref[...] = up.reshape(BLOCKS, 8, SPEC)
    spec_ref[...] = jnp.zeros(spec_ref.shape, F32)
    for doc in range(DOCS):
        start, end = doc_bounds(spans_ref, doc)

        @pl.loop(0, (end - start + TILE - 1) // TILE)
        def _(tile):
            first = start + TILE * tile

            def step(n, sums):
                sums = list(sums)
                place = 0
                for re_lanes, im_lanes in columns():
                    u_re = up_ref[n, :, re_lanes]
                    u_im = up_ref[n, :, im_lanes]
                    for i in range(TILE):
                        g_re = taps_ref[n - first - i + PAD, :, re_lanes]
                        g_im = taps_ref[n - first - i + PAD, :, im_lanes]
                        sums[place] += g_re * u_re + g_im * u_im
                        sums[place + 1] += g_re * u_im - g_im * u_re
                        place += 2
                return tuple(sums)

            sums = lax.fori_loop(first, end, step, tuple(zero_sums()))
            store_tile(spec_ref, first, sums)

    lag_ref[pl.ds(BLOCKS, 1)] = jnp.zeros((1, 8, SPEC), F32)

    @pl.loop(0, BLOCKS // TILE)
    def _(tile):
        first = TILE * tile
        sums = tuple(zero_sums())
        for doc in range(DOCS):
            start, end = doc_bounds(spans_ref, doc)
            shift = PAD * (doc + 1)

            def step(n, sums):
                sums = list(sums)
                place = 0
                for re_lanes, im_lanes in columns():
                    u_re = up_ref[n, :, re_lanes]
                    u_im = up_ref[n, :, im_lanes]
                    for i in range(TILE):
                        z_re = source_ref[n - first - i + shift, :, re_lanes]
                        z_im = source_ref[n - first - i + shift, :, im_lanes]
                        sums[place] += z_re * u_re + z_im * u_im
                        sums[place + 1] += z_re * u_im - z_im * u_re
                        place += 2
                return tuple(sums)

            sums = lax.fori_loop(start + first, end, step, sums)
        store_tile(lag_ref, first, sums)

    source_grad = from_spectrum(spec_ref[pl.ds(0, BLOCKS)].reshape(BLOCKS * 8, SPEC), inverse_ref)
    lags, later = lag_ref[pl.ds(0, BLOCKS)], lag_ref[pl.ds(1, BLOCKS)]
    folded = jnp.concatenate(
        [
            lags[..., :FREQS] + signs * later[..., FREQS:],
            lags[..., FREQS:] - signs * later[..., :FREQS],
        ],
        axis=2,
    )
    tap_grad = from_spectrum(folded.reshape(BLOCKS * 8, SPEC), inverse_ref)
    out_ref[...] = jnp.concatenate(
        [
            sender_slabs(source_grad * (1.0 / BLOCK), 8),
            sender_slabs(tap_grad * (TOKENS**-0.5 / BLOCK), 8),
        ],
        axis=1,
    ).astype(BF16)


def product_kernel(slabs_ref, values_ref, gate_ref, gate_grad_ref, values_grad_ref, filter_grad_ref):
    tokens, width = values_ref.shape
    slabs = slabs_ref[...].astype(F32)
    gated_grad = slabs[:, :8].reshape(width, tokens).T
    gate_grad_ref[...] = (gated_grad * values_ref[...].astype(F32)).astype(BF16)
    values_grad_ref[...] = (gated_grad * gate_ref[...].astype(F32)).astype(BF16)
    filter_grad_ref[...] = slabs[:, 8:].reshape(width, tokens).T


def call(kernel, out_shape, scratch=(), smem_first=False, cost=4_000_000):
    vmem = pl.BlockSpec(memory_space=pltpu.VMEM)

    def run(*operands):
        specs = [vmem] * len(operands)
        if smem_first:
            specs[0] = pl.BlockSpec(memory_space=pltpu.SMEM)
        outs = jax.tree.map(lambda _: vmem, out_shape)
        return pl.pallas_call(
            kernel,
            out_shape=out_shape,
            in_specs=specs,
            out_specs=outs,
            scratch_shapes=list(scratch),
            compiler_params=pltpu.CompilerParams(vmem_limit_bytes=VMEM_LIMIT),
            cost_estimate=pl.CostEstimate(flops=cost, bytes_accessed=cost, transcendentals=0),
        )(*operands)

    return run


def exchange(array, axis):
    return lax.all_to_all(array, axis, split_axis=0, concat_axis=0, tiled=True)


def shards(input_gate, output_gate, values, residual, cotangent, filters, norm_gain, doc_spans):
    tokens, width = input_gate.shape
    shape = jax.ShapeDtypeStruct
    table, inverse = (jnp.asarray(t) for t in window_tables())
    spans = doc_spans.reshape(2 * DOCS)
    gain = norm_gain.reshape(1, width)
    like = shape((tokens, width), BF16)
    wide = shape((tokens, width), F32)
    pair = shape((64, 16, tokens), BF16)
    single = shape((64, 8, tokens), BF16)

    outgoing = call(gate_kernel, pair)(values, input_gate, filters)
    incoming = exchange(outgoing, "seq")
    conv, source, taps = call(
        forward_kernel,
        (single, shape((ROWS, 8, SPEC), F32), shape((PAD + BLOCKS, 8, SPEC), F32)),
        scratch=[pltpu.VMEM((PAD + BLOCKS, 8, SPEC), F32)],
        smem_first=True,
    )(spans, incoming, table, inverse)
    conv = exchange(conv, "seq")
    mixed, token_conv, sums = call(mixed_kernel, (wide, like, shape((8, 8, tokens), F32)))(
        conv, residual, output_gate, cotangent, gain
    )
    sums = exchange(sums, "chan")
    conv_grad = call(grad_kernel, single)(sums, mixed, output_gate, cotangent, gain)
    conv_grad = exchange(conv_grad, "seq")
    normed, residual_grad, output_gate_grad = call(token_kernel, (like, like, like))(
        sums, mixed, token_conv, cotangent, gain
    )
    grads = call(
        backward_kernel,
        pair,
        scratch=[
            pltpu.VMEM((BLOCKS, 8, SPEC), F32),
            pltpu.VMEM((BLOCKS + PAD, 8, SPEC), F32),
            pltpu.VMEM((BLOCKS + PAD, 8, SPEC), F32),
        ],
        smem_first=True,
    )(spans, conv_grad, source, taps, table, inverse)
    grads = exchange(grads, "seq")
    input_gate_grad, values_grad, filter_grad = call(product_kernel, (like, like, wide))(
        grads, values, input_gate
    )
    return (normed, residual_grad, input_gate_grad, output_gate_grad, values_grad, filter_grad)


def solution(mesh):
    split = P("seq", "chan")
    return jax.shard_map(
        shards,
        mesh=mesh,
        in_specs=(split, split, split, split, split, split, P("chan"), P()),
        out_specs=(split,) * 6,
        check_vma=False,
    )
```

```python
import jax
import jax.numpy as jnp
import ml_dtypes
import numpy as np
from jax import lax
from jax.experimental import pallas as pl
from jax.experimental.pallas import tpu as pltpu
from jax.sharding import PartitionSpec as P

D = 4096
BLOCK = 512
TOKENS = 16384
DOCS = 4
EPSILON = 1e-06
BLOCKS = TOKENS // BLOCK
FREQS = BLOCK
SPEC = 2 * FREQS
TILE = 4
PAD = TILE
ROWS = BLOCKS + PAD * (DOCS + 2)
LAG_PAD = 2 * TILE
LAG_ROWS = LAG_PAD + BLOCKS + TILE
TRIPLE = 2 * FREQS
F32 = jnp.float32
BF16 = jnp.bfloat16


def split_bf16(array):
    high = array.astype(ml_dtypes.bfloat16)
    low = (array - high.astype(np.float64)).astype(ml_dtypes.bfloat16)
    return np.stack([high, low])


def window_table():
    places = np.arange(BLOCK, dtype=np.int64)
    odd = 2 * np.arange(FREQS, dtype=np.int64) + 1
    phase = (places[:, None] * odd[None, :] % (4 * BLOCK)) * (np.pi / (2 * BLOCK))
    forward = np.concatenate([np.cos(phase), -np.sin(phase)], axis=1)
    return split_bf16(forward)


def half_signs():
    lanes = lax.broadcasted_iota(jnp.int32, (1, 1, FREQS), 2)
    return (1 - 2 * (lanes % 2)).astype(F32)


def block_rows(slabs):
    count, chans, width = slabs.shape
    pairs = slabs.reshape(count // 2, 2, chans, width)
    joined = jnp.concatenate([pairs[:, 0], pairs[:, 1]], axis=2)
    return joined.reshape(count // 2 * chans, 2 * width)


def sender_slabs(rows, chans):
    width = rows.shape[1] // 2
    blocks = rows.reshape(rows.shape[0] // chans, 1, chans, 2 * width)
    joined = jnp.concatenate([blocks[..., :width], blocks[..., width:]], axis=1)
    return joined.reshape(2 * blocks.shape[0], chans, width)


def to_spectrum(rows, table_ref):
    rows = rows.astype(BF16)
    high = jnp.dot(rows, table_ref[0], preferred_element_type=F32)
    return high + jnp.dot(rows, table_ref[1], preferred_element_type=F32)


def from_spectrum(spec, table_ref):
    high = spec.astype(BF16)
    low = (spec - high.astype(F32)).astype(BF16)
    across = (((1,), (1,)), ((), ()))
    total = lax.dot_general(high, table_ref[0], across, preferred_element_type=F32)
    total += lax.dot_general(low, table_ref[0], across, preferred_element_type=F32)
    return total + lax.dot_general(high, table_ref[1], across, preferred_element_type=F32)


def doc_bounds(spans_ref, doc):
    return spans_ref[2 * doc] // BLOCK, spans_ref[2 * doc + 1] // BLOCK


def triple_lanes(lane):
    return tuple(pl.ds(part * FREQS + lane, 128) for part in range(2))


def store_triple(ref, rows, real, imag):
    ref[rows, :, pl.ds(0, FREQS)] = real
    ref[rows, :, pl.ds(FREQS, FREQS)] = imag


def load_triple(ref, row, lane):
    return tuple(ref[row, :, lanes] for lanes in triple_lanes(lane))


COLUMNS = 4


def lane_groups():
    for lane in range(0, FREQS, 128 * COLUMNS):
        yield [lane + 128 * k for k in range(COLUMNS)]


def load_source(ref, row, lane):
    return load_triple(ref, row, lane)


def zero_sums():
    return tuple(jnp.zeros((8, 128), F32) for _ in range(2 * TILE))


def plain_sums(others, window, sums):
    sums = list(sums)
    for j, (a, b) in enumerate(others):
        for i in range(TILE):
            c, d = window[TILE - 1 + i - j]
            sums[2 * i] += c * a - d * b
            sums[2 * i + 1] += c * b + d * a
    return tuple(sums)


def conj_sums(others, window, sums):
    sums = list(sums)
    for j, (a, b) in enumerate(others):
        for i in range(TILE):
            c, d = window[TILE - 1 + j - i]
            sums[2 * i] += c * a + d * b
            sums[2 * i + 1] += c * b - d * a
    return tuple(sums)


def store_plain(ref, row, lane, sums):
    for i in range(TILE):
        ref[row + i, :, pl.ds(lane, 128)] = sums[2 * i]
        ref[row + i, :, pl.ds(FREQS + lane, 128)] = sums[2 * i + 1]


def store_conj(ref, row, lane, sums):
    for i in range(TILE):
        ref[row + i, :, pl.ds(lane, 128)] = sums[2 * i]
        ref[row + i, :, pl.ds(FREQS + lane, 128)] = sums[2 * i + 1]


def steps(length):
    return (jnp.maximum(length, 0) + TILE - 1) // TILE


CHUNKS = 4


def gate_kernel(values_hbm, gate_hbm, filters_hbm, out_hbm, values_ref, gate_ref, filters_ref, out_ref, sems, out_sems):
    width = values_ref.shape[1] // CHUNKS
    slabs, twice, tokens = out_ref.shape
    slabs //= CHUNKS
    shape = (slabs, twice // 2, tokens)
    arriving = []
    for chunk in range(CHUNKS):
        lanes = pl.ds(chunk * width, width)
        arriving.append(
            [
                pltpu.make_async_copy(hbm.at[:, lanes], ref.at[:, lanes], sems.at[k, chunk])
                for k, (hbm, ref) in enumerate(
                    ((values_hbm, values_ref), (gate_hbm, gate_ref), (filters_hbm, filters_ref))
                )
            ]
        )
        for copy in arriving[-1]:
            copy.start()
    leaving = []
    for chunk in range(CHUNKS):
        lanes, rows = pl.ds(chunk * width, width), pl.ds(chunk * slabs, slabs)
        for copy in arriving[chunk]:
            copy.wait()
        gated = values_ref[:, lanes].astype(F32) * gate_ref[:, lanes].astype(F32)
        both = jnp.concatenate(
            [gated.T.reshape(shape), filters_ref[:, lanes].T.reshape(shape)], axis=1
        )
        out_ref[rows] = both.astype(BF16)
        leaving.append(pltpu.make_async_copy(out_ref.at[rows], out_hbm.at[rows], out_sems.at[chunk]))
        leaving[-1].start()
    for copy in leaving:
        copy.wait()


def stage_kernel(residual_hbm, gate_hbm, cotangent_hbm, staged_ref, sems):
    copies = [
        pltpu.make_async_copy(hbm, staged_ref.at[k], sems.at[k])
        for k, hbm in enumerate((residual_hbm, gate_hbm, cotangent_hbm))
    ]
    for copy in copies:
        copy.start()
    for copy in copies:
        copy.wait()


def forward_kernel(spans_ref, slabs_ref, table_ref, conv_hbm, source_hbm, taps_hbm, conv_ref, source_ref, taps_ref, spec_ref, sems):
    slabs = slabs_ref[...].astype(F32)
    signs = half_signs()
    source = to_spectrum(block_rows(slabs[:, :8]), table_ref).reshape(BLOCKS, 8, SPEC)
    spec_ref[pl.ds(0, BLOCKS)] = source
    taps = to_spectrum(block_rows(slabs[:, 8:]), table_ref).reshape(BLOCKS, 8, SPEC)
    real, imag = taps[..., :FREQS], taps[..., FREQS:]
    nothing = jnp.zeros((1, 8, FREQS), F32)
    before_real = jnp.concatenate([nothing, real[:-1]], axis=0)
    before_imag = jnp.concatenate([nothing, imag[:-1]], axis=0)
    taps_ref[pl.ds(0, LAG_PAD)] = jnp.zeros((LAG_PAD, 8, TRIPLE), F32)
    taps_ref[pl.ds(LAG_PAD + BLOCKS, TILE)] = jnp.zeros((TILE, 8, TRIPLE), F32)
    store_triple(taps_ref, pl.ds(LAG_PAD, BLOCKS), real - signs * before_imag, imag + signs * before_real)
    source_ref[...] = jnp.zeros((ROWS, 8, TRIPLE), F32)
    for doc in range(DOCS):
        start, end = doc_bounds(spans_ref, doc)

        @pl.loop(start, end)
        def _(n):
            row = spec_ref[n]
            store_triple(source_ref, n + PAD * (doc + 1), row[:, :FREQS], row[:, FREQS:])

    kept = [
        pltpu.make_async_copy(source_ref, source_hbm, sems.at[0]),
        pltpu.make_async_copy(taps_ref, taps_hbm, sems.at[1]),
    ]
    for copy in kept:
        copy.start()
    spec_ref[...] = jnp.zeros(spec_ref.shape, F32)
    for doc in reversed(range(DOCS)):
        start, end = doc_bounds(spans_ref, doc)
        shift = PAD * (doc + 1)

        @pl.loop(0, steps(end - start))
        def _(tile):
            first = end - TILE * (tile + 1)
            for lanes in lane_groups():

                def step(group, sums):
                    s = start + TILE * group
                    out = []
                    for lane, part in zip(lanes, sums):
                        window = [
                            load_triple(taps_ref, first - s + LAG_PAD + k - (TILE - 1), lane)
                            for k in range(2 * TILE - 1)
                        ]
                        others = [load_source(source_ref, s + j + shift, lane) for j in range(TILE)]
                        out.append(plain_sums(others, window, part))
                    return tuple(out)

                sums = lax.fori_loop(0, steps(first + TILE - start), step, tuple(zero_sums() for _ in lanes))
                for lane, part in zip(lanes, sums):
                    store_plain(spec_ref, first + PAD, lane, part)

    total = spec_ref[pl.ds(PAD, BLOCKS)].reshape(BLOCKS * 8, SPEC)
    conv = from_spectrum(total, table_ref) * (1.0 / BLOCK)
    conv_ref[...] = sender_slabs(conv, 8).astype(BF16)
    leaving = pltpu.make_async_copy(conv_ref, conv_hbm, sems.at[2])
    leaving.start()
    for copy in (*kept, leaving):
        copy.wait()


def mixed_kernel(conv_ref, staged_ref, gain_ref, mixed_ref, sums_ref):
    _, tokens, width = staged_ref.shape
    conv = conv_ref[...].astype(F32).reshape(width, tokens).T
    mixed = staged_ref[0].astype(F32) + conv * staged_ref[1].astype(F32)
    lifted = staged_ref[2].astype(F32) * gain_ref[...].astype(F32)
    mixed_ref[0] = mixed
    mixed_ref[1] = conv
    power = jnp.sum(mixed * mixed, axis=1, keepdims=True)
    inner = jnp.sum(lifted * mixed, axis=1, keepdims=True)
    lanes = lax.broadcasted_iota(jnp.int32, (tokens, 128), 1)
    both = jnp.where(lanes == 0, power, jnp.where(lanes == 1, inner, 0.0)).T[:8]
    sums_ref[...] = jnp.broadcast_to(both[None], sums_ref.shape)


def token_scales(sums_ref):
    total = jnp.sum(sums_ref[...], axis=0)
    padded = jnp.concatenate([total, jnp.zeros((120, total.shape[1]), F32)], axis=0).T
    scale = lax.rsqrt(padded[:, 0:1] / D + EPSILON)
    return scale, padded[:, 1:2] / D


def grad_kernel(sums_ref, mixed_ref, staged_ref, gain_ref, grad_ref):
    scale, inner = token_scales(sums_ref)
    lifted = staged_ref[2].astype(F32) * gain_ref[...].astype(F32)
    mixed_grad = scale * (lifted - mixed_ref[0] * (scale * scale * inner))
    conv_grad = mixed_grad * staged_ref[1].astype(F32)
    grad_ref[...] = conv_grad.T.reshape(grad_ref.shape).astype(BF16)


def token_kernel(sums_ref, mixed_ref, staged_ref, gain_ref, normed_ref, residual_grad_ref, gate_grad_ref):
    scale, inner = token_scales(sums_ref)
    gain = gain_ref[...].astype(F32)
    mixed = mixed_ref[0]
    lifted = staged_ref[2].astype(F32) * gain
    normed_ref[...] = (mixed * scale * gain).astype(BF16)
    mixed_grad = scale * (lifted - mixed * (scale * scale * inner))
    residual_grad_ref[...] = mixed_grad.astype(BF16)
    gate_grad_ref[...] = (mixed_grad * mixed_ref[1]).astype(BF16)


def backward_kernel(spans_ref, slabs_ref, source_hbm, taps_hbm, table_ref, out_ref, source_ref, taps_ref, up_ref, spec_ref, lag_ref, sems):
    kept = [
        pltpu.make_async_copy(source_hbm, source_ref, sems.at[0]),
        pltpu.make_async_copy(taps_hbm, taps_ref, sems.at[1]),
    ]
    for copy in kept:
        copy.start()
    signs = half_signs()
    up = to_spectrum(block_rows(slabs_ref[...].astype(F32)), table_ref)
    spec_ref[pl.ds(0, BLOCKS)] = up.reshape(BLOCKS, 8, SPEC)
    up_ref[...] = jnp.zeros((ROWS, 8, SPEC), F32)
    for doc in range(DOCS):
        start, end = doc_bounds(spans_ref, doc)

        @pl.loop(start, end)
        def _(n):
            up_ref[n + PAD * (doc + 1)] = spec_ref[n]

    for copy in kept:
        copy.wait()

    def load_up(row, lane):
        return [
            (up_ref[row + j, :, pl.ds(lane, 128)], up_ref[row + j, :, pl.ds(FREQS + lane, 128)])
            for j in range(TILE)
        ]

    spec_ref[...] = jnp.zeros(spec_ref.shape, F32)
    for doc in range(DOCS):
        start, end = doc_bounds(spans_ref, doc)
        shift = PAD * (doc + 1)

        @pl.loop(0, steps(end - start))
        def _(tile):
            first = start + TILE * tile
            for lanes in lane_groups():

                def step(group, sums):
                    n = TILE * group
                    out = []
                    for lane, part in zip(lanes, sums):
                        window = [
                            load_triple(taps_ref, n + LAG_PAD + k - (TILE - 1), lane)
                            for k in range(2 * TILE - 1)
                        ]
                        out.append(conj_sums(load_up(first + n + shift, lane), window, part))
                    return tuple(out)

                sums = lax.fori_loop(0, steps(end - first), step, tuple(zero_sums() for _ in lanes))
                for lane, part in zip(lanes, sums):
                    store_conj(spec_ref, first, lane, part)

    lag_ref[pl.ds(BLOCKS, 1)] = jnp.zeros((1, 8, SPEC), F32)

    @pl.loop(0, BLOCKS // TILE)
    def _(tile):
        first = TILE * tile
        for lanes in lane_groups():
            sums = tuple(zero_sums() for _ in lanes)
            for doc in range(DOCS):
                start, end = doc_bounds(spans_ref, doc)
                begin = start + PAD * (doc + 1)

                def step(group, sums):
                    n = begin + TILE * group
                    out = []
                    for lane, part in zip(lanes, sums):
                        window = [
                            load_triple(source_ref, n + k - (TILE - 1), lane)
                            for k in range(2 * TILE - 1)
                        ]
                        out.append(conj_sums(load_up(n + first, lane), window, part))
                    return tuple(out)

                sums = lax.fori_loop(0, steps(end - start - first), step, sums)
            for lane, part in zip(lanes, sums):
                store_conj(lag_ref, first, lane, part)

    source_grad = from_spectrum(spec_ref[pl.ds(0, BLOCKS)].reshape(BLOCKS * 8, SPEC), table_ref)
    lags, later = lag_ref[pl.ds(0, BLOCKS)], lag_ref[pl.ds(1, BLOCKS)]
    folded = jnp.concatenate(
        [
            lags[..., :FREQS] + signs * later[..., FREQS:],
            lags[..., FREQS:] - signs * later[..., :FREQS],
        ],
        axis=2,
    )
    tap_grad = from_spectrum(folded.reshape(BLOCKS * 8, SPEC), table_ref)
    out_ref[...] = jnp.concatenate(
        [
            sender_slabs(source_grad * (1.0 / BLOCK), 8),
            sender_slabs(tap_grad * (TOKENS**-0.5 / BLOCK), 8),
        ],
        axis=1,
    ).astype(BF16)


def product_kernel(slabs_ref, values_ref, gate_ref, gate_grad_hbm, values_grad_hbm, filter_grad_hbm, gate_grad_ref, values_grad_ref, filter_grad_ref, sems):
    tokens, width = values_ref.shape
    part = tokens // 2
    leaving = []
    for k in range(2):
        rows = pl.ds(k * part, part)
        slabs = slabs_ref[:, :, rows].astype(F32)
        gated_grad = slabs[:, :8].reshape(width, part).T
        filter_grad_ref[rows] = slabs[:, 8:].reshape(width, part).T
        gate_grad_ref[rows] = (gated_grad * values_ref[rows].astype(F32)).astype(BF16)
        values_grad_ref[rows] = (gated_grad * gate_ref[rows].astype(F32)).astype(BF16)
        for which, (ref, hbm) in enumerate(
            (
                (filter_grad_ref, filter_grad_hbm),
                (gate_grad_ref, gate_grad_hbm),
                (values_grad_ref, values_grad_hbm),
            )
        ):
            leaving.append(pltpu.make_async_copy(ref.at[rows], hbm.at[rows], sems.at[which, k]))
            leaving[-1].start()
    for copy in leaving:
        copy.wait()


def call(kernel, ins, outs, scratch=(), limit=16, cost=4_000_000):
    spaces = {"v": pltpu.VMEM, "h": pltpu.HBM, "s": pltpu.SMEM}
    spec = lambda space: pl.BlockSpec(memory_space=spaces[space])
    return pl.pallas_call(
        kernel,
        out_shape=[
            pltpu.HBM(*shape) if space == "h" else jax.ShapeDtypeStruct(*shape)
            for shape, space in outs
        ],
        in_specs=[spec(space) for space in ins],
        out_specs=[spec(space) for _, space in outs],
        scratch_shapes=list(scratch),
        compiler_params=pltpu.CompilerParams(vmem_limit_bytes=limit * 1024 * 1024),
        cost_estimate=pl.CostEstimate(flops=cost, bytes_accessed=cost, transcendentals=0),
    )


def in_hbm(*arrays):
    return [pltpu.with_memory_space_constraint(array, pltpu.HBM) for array in arrays]


def exchange(array, axis):
    return lax.all_to_all(array, axis, split_axis=0, concat_axis=0, tiled=True)


def body(exchange, input_gate, output_gate, values, residual, cotangent, filters, gain, spans):
    tokens, width = input_gate.shape
    table = jnp.asarray(window_table())
    like, wide = ((tokens, width), BF16), ((tokens, width), F32)
    pair, single = ((64, 16, tokens), BF16), ((64, 8, tokens), BF16)
    source_rows, lag_rows = ((ROWS, 8, TRIPLE), F32), ((LAG_ROWS, 8, TRIPLE), F32)
    sums_rows = ((8, 8, tokens), F32)
    dma = pltpu.SemaphoreType.DMA
    vmem = lambda shape: pltpu.VMEM(*shape)

    (outgoing,) = call(
        gate_kernel,
        "hhh",
        [(pair, "h")],
        [vmem(like), vmem(like), vmem(wide), vmem(pair), dma((3, CHUNKS)), dma((CHUNKS,))],
    )(*in_hbm(values, input_gate, filters))
    incoming = exchange(outgoing, "seq")
    conv, source, taps = call(
        forward_kernel,
        "svv",
        [(single, "h"), (source_rows, "h"), (lag_rows, "h")],
        [vmem(single), vmem(source_rows), vmem(lag_rows), pltpu.VMEM((PAD + BLOCKS, 8, SPEC), F32), dma((3,))],
        limit=24,
    )(spans, incoming, table)
    conv = exchange(conv, "seq")
    (staged,) = call(stage_kernel, "hhh", [(((3, tokens, width), BF16), "v")], [dma((3,))])(
        *in_hbm(residual, output_gate, cotangent)
    )
    mixed, sums = call(
        mixed_kernel, "vvv", [(((2, tokens, width), F32), "v"), (sums_rows, "v")]
    )(conv, staged, gain)
    sums = exchange(sums, "chan")
    (conv_grad,) = call(grad_kernel, "vvvv", [(single, "v")])(sums, mixed, staged, gain)
    conv_grad = exchange(conv_grad, "seq")
    normed, residual_grad, output_gate_grad = call(token_kernel, "vvvv", [(like, "v")] * 3)(
        sums, mixed, staged, gain
    )
    conv_grad, normed = lax.optimization_barrier((conv_grad, normed))
    (grads,) = call(
        backward_kernel,
        "svhhv",
        [(pair, "v")],
        [
            vmem(source_rows),
            vmem(lag_rows),
            pltpu.VMEM((ROWS, 8, SPEC), F32),
            pltpu.VMEM((BLOCKS + PAD, 8, SPEC), F32),
            pltpu.VMEM((BLOCKS + PAD, 8, SPEC), F32),
            dma((2,)),
        ],
        limit=24,
    )(spans, conv_grad, *in_hbm(source, taps), table)
    grads = exchange(grads, "seq")
    input_gate_grad, values_grad, filter_grad = call(
        product_kernel,
        "vvv",
        [(like, "h"), (like, "h"), (wide, "h")],
        [vmem(like), vmem(like), vmem(wide), dma((3, 2))],
    )(grads, values, input_gate)
    return (normed, residual_grad, input_gate_grad, output_gate_grad, values_grad, filter_grad)


def shards(input_gate, output_gate, values, residual, cotangent, filters, norm_gain, doc_spans):
    gain = norm_gain.reshape(1, norm_gain.shape[0])
    spans = doc_spans.reshape(2 * DOCS)
    return body(exchange, input_gate, output_gate, values, residual, cotangent, filters, gain, spans)


def solution(mesh):
    split = P("seq", "chan")
    return jax.shard_map(
        shards,
        mesh=mesh,
        in_specs=(split, split, split, split, split, split, P("chan"), P()),
        out_specs=(split,) * 6,
        check_vma=False,
    )
```

```python
import jax
import jax.numpy as jnp
import ml_dtypes
import numpy as np
from jax import lax
from jax.experimental import pallas as pl
from jax.experimental.pallas import tpu as pltpu
from jax.sharding import PartitionSpec as P

D = 4096
BLOCK = 512
TOKENS = 16384
DOCS = 4
EPSILON = 1e-06
BLOCKS = TOKENS // BLOCK
FREQS = BLOCK
SPEC = 2 * FREQS
TILE = 4
PAD = TILE
ROWS = BLOCKS + PAD * (DOCS + 2)
LAG_PAD = TILE
LAG_ROWS = LAG_PAD + BLOCKS
F32 = jnp.float32
BF16 = jnp.bfloat16


def split_bf16(array):
    high = array.astype(ml_dtypes.bfloat16)
    low = (array - high.astype(np.float64)).astype(ml_dtypes.bfloat16)
    return np.stack([high, low])


def window_table():
    places = np.arange(BLOCK, dtype=np.int64)
    odd = 2 * np.arange(FREQS, dtype=np.int64) + 1
    phase = (places[:, None] * odd[None, :] % (4 * BLOCK)) * (np.pi / (2 * BLOCK))
    forward = np.concatenate([np.cos(phase), -np.sin(phase)], axis=1)
    return split_bf16(forward)


def half_signs():
    lanes = lax.broadcasted_iota(jnp.int32, (1, 1, FREQS), 2)
    return (1 - 2 * (lanes % 2)).astype(F32)


def block_rows(slabs):
    count, chans, width = slabs.shape
    pairs = slabs.reshape(count // 2, 2, chans, width)
    joined = jnp.concatenate([pairs[:, 0], pairs[:, 1]], axis=2)
    return joined.reshape(count // 2 * chans, 2 * width)


def sender_slabs(rows, chans):
    width = rows.shape[1] // 2
    blocks = rows.reshape(rows.shape[0] // chans, 1, chans, 2 * width)
    joined = jnp.concatenate([blocks[..., :width], blocks[..., width:]], axis=1)
    return joined.reshape(2 * blocks.shape[0], chans, width)


def to_spectrum(rows, table_ref):
    rows = rows.astype(BF16)
    high = jnp.dot(rows, table_ref[0], preferred_element_type=F32)
    return high + jnp.dot(rows, table_ref[1], preferred_element_type=F32)


def from_spectrum(spec, table_ref):
    high = spec.astype(BF16)
    low = (spec - high.astype(F32)).astype(BF16)
    across = (((1,), (1,)), ((), ()))
    total = lax.dot_general(high, table_ref[0], across, preferred_element_type=F32)
    return total + lax.dot_general(low, table_ref[0], across, preferred_element_type=F32)


def doc_bounds(spans_ref, doc):
    return spans_ref[2 * doc] // BLOCK, spans_ref[2 * doc + 1] // BLOCK


COLUMNS = range(0, FREQS, 128)


def load(ref, row):
    return [(ref[row, :, pl.ds(lane, 128)], ref[row, :, pl.ds(FREQS + lane, 128)]) for lane in COLUMNS]


def store_tile(ref, row, sums):
    for lane, column in zip(COLUMNS, sums):
        for i, (real, imag) in enumerate(column):
            ref[row + i, :, pl.ds(lane, 128)] = real
            ref[row + i, :, pl.ds(FREQS + lane, 128)] = imag


def zero_sums():
    zero = jnp.zeros((8, 128), F32)
    return tuple(tuple((zero, zero) for _ in range(TILE)) for _ in COLUMNS)


def add_rows(sums, rows_ref, rows, taps_ref, tap, conj, triangle=False):
    out = []
    for lane, column in zip(COLUMNS, sums):
        re_lanes, im_lanes = pl.ds(lane, 128), pl.ds(FREQS + lane, 128)
        column, seen = list(column), {}
        for j, row in enumerate(rows):
            a, b = rows_ref[row, :, re_lanes], rows_ref[row, :, im_lanes]
            for i in range(TILE):
                offset = j - i if conj else i - j
                if triangle and offset < 0:
                    continue
                if offset not in seen:
                    seen[offset] = (taps_ref[tap + offset, :, re_lanes], taps_ref[tap + offset, :, im_lanes])
                c, d = seen[offset]
                real, imag = column[i]
                if conj:
                    column[i] = (real + (c * a + d * b), imag + (c * b - d * a))
                else:
                    column[i] = (real + (c * a - d * b), imag + (c * b + d * a))
        out.append(tuple(column))
    return tuple(out)


def add_range(sums, count, step):
    count = jnp.maximum(count, 0)
    full = count // TILE
    sums = lax.fori_loop(0, full, lambda g, sums: step(sums, TILE * g, TILE), sums)
    return lax.fori_loop(TILE * full, count, lambda k, sums: step(sums, k, 1), sums)


def tiles(length):
    return (length + TILE - 1) // TILE


CHUNKS = 4


def gate_kernel(values_hbm, gate_hbm, filters_hbm, out_hbm, values_ref, gate_ref, filters_ref, out_ref, sems, out_sems):
    width = values_ref.shape[1] // CHUNKS
    slabs, twice, tokens = out_ref.shape
    slabs //= CHUNKS
    shape = (slabs, twice // 2, tokens)
    arriving = []
    for chunk in range(CHUNKS):
        lanes = pl.ds(chunk * width, width)
        arriving.append(
            [
                pltpu.make_async_copy(hbm.at[:, lanes], ref.at[:, lanes], sems.at[k, chunk])
                for k, (hbm, ref) in enumerate(
                    ((values_hbm, values_ref), (gate_hbm, gate_ref), (filters_hbm, filters_ref))
                )
            ]
        )
        for copy in arriving[-1]:
            copy.start()
    leaving = []
    for chunk in range(CHUNKS):
        lanes, rows = pl.ds(chunk * width, width), pl.ds(chunk * slabs, slabs)
        for copy in arriving[chunk]:
            copy.wait()
        gated = values_ref[:, lanes].astype(F32) * gate_ref[:, lanes].astype(F32)
        both = jnp.concatenate(
            [gated.T.reshape(shape), filters_ref[:, lanes].T.reshape(shape)], axis=1
        )
        out_ref[rows] = both.astype(BF16)
        leaving.append(pltpu.make_async_copy(out_ref.at[rows], out_hbm.at[rows], out_sems.at[chunk]))
        leaving[-1].start()
    for copy in leaving:
        copy.wait()


def stage_kernel(residual_hbm, gate_hbm, cotangent_hbm, staged_ref, sems):
    copies = [
        pltpu.make_async_copy(hbm, staged_ref.at[k], sems.at[k])
        for k, hbm in enumerate((residual_hbm, gate_hbm, cotangent_hbm))
    ]
    for copy in copies:
        copy.start()
    for copy in copies:
        copy.wait()


def forward_kernel(spans_ref, slabs_ref, table_ref, conv_ref, source_hbm, taps_hbm, source_ref, taps_ref, spec_ref, sems):
    slabs = slabs_ref[...].astype(F32)
    signs = half_signs()
    source = to_spectrum(block_rows(slabs[:, :8]), table_ref).reshape(BLOCKS, 8, SPEC)
    spec_ref[pl.ds(0, BLOCKS)] = source
    taps = to_spectrum(block_rows(slabs[:, 8:]), table_ref).reshape(BLOCKS, 8, SPEC)
    real, imag = taps[..., :FREQS], taps[..., FREQS:]
    nothing = jnp.zeros((1, 8, FREQS), F32)
    before_real = jnp.concatenate([nothing, real[:-1]], axis=0)
    before_imag = jnp.concatenate([nothing, imag[:-1]], axis=0)
    taps_ref[pl.ds(0, LAG_PAD)] = jnp.zeros((LAG_PAD, 8, SPEC), F32)
    taps_ref[pl.ds(LAG_PAD, BLOCKS), :, :FREQS] = real - signs * before_imag
    taps_ref[pl.ds(LAG_PAD, BLOCKS), :, FREQS:] = imag + signs * before_real
    source_ref[...] = jnp.zeros((ROWS, 8, SPEC), F32)
    for doc in range(DOCS):
        start, end = doc_bounds(spans_ref, doc)

        @pl.loop(start, end)
        def _(n):
            source_ref[n + PAD * (doc + 1)] = spec_ref[n]

    kept = [
        pltpu.make_async_copy(source_ref, source_hbm, sems.at[0]),
        pltpu.make_async_copy(taps_ref, taps_hbm, sems.at[1]),
    ]
    for copy in kept:
        copy.start()
    spec_ref[...] = jnp.zeros(spec_ref.shape, F32)
    for doc in reversed(range(DOCS)):
        start, end = doc_bounds(spans_ref, doc)
        shift = PAD * (doc + 1)

        @pl.loop(0, tiles(end - start))
        def _(tile):
            first = end - TILE * (tile + 1)

            def step(sums, k, count):
                s = first - k - count
                rows = [s + shift + j for j in range(count)]
                return add_rows(sums, source_ref, rows, taps_ref, first - s + LAG_PAD, False)

            rows = [first + shift + j for j in range(TILE)]
            sums = add_rows(zero_sums(), source_ref, rows, taps_ref, LAG_PAD, False, triangle=True)
            store_tile(spec_ref, first + PAD, add_range(sums, first - start, step))

    total = spec_ref[pl.ds(PAD, BLOCKS)].reshape(BLOCKS * 8, SPEC)
    conv = from_spectrum(total, table_ref) * (1.0 / BLOCK)
    conv_ref[...] = sender_slabs(conv, 8).astype(BF16)
    for copy in kept:
        copy.wait()


def mixed_kernel(conv_ref, staged_ref, gain_ref, mixed_ref, sums_ref):
    _, tokens, width = staged_ref.shape
    conv = conv_ref[...].astype(F32).reshape(width, tokens).T
    mixed = staged_ref[0].astype(F32) + conv * staged_ref[1].astype(F32)
    lifted = staged_ref[2].astype(F32) * gain_ref[...].astype(F32)
    mixed_ref[0] = mixed
    mixed_ref[1] = conv
    power = jnp.sum(mixed * mixed, axis=1, keepdims=True)
    inner = jnp.sum(lifted * mixed, axis=1, keepdims=True)
    lanes = lax.broadcasted_iota(jnp.int32, (tokens, 128), 1)
    both = jnp.where(lanes == 0, power, jnp.where(lanes == 1, inner, 0.0)).T[:8]
    sums_ref[...] = jnp.broadcast_to(both[None], sums_ref.shape)


def token_scales(sums_ref):
    total = jnp.sum(sums_ref[...], axis=0)
    padded = jnp.concatenate([total, jnp.zeros((120, total.shape[1]), F32)], axis=0).T
    scale = lax.rsqrt(padded[:, 0:1] / D + EPSILON)
    return scale, padded[:, 1:2] / D


def grad_kernel(sums_ref, mixed_ref, staged_ref, gain_ref, grad_ref):
    scale, inner = token_scales(sums_ref)
    lifted = staged_ref[2].astype(F32) * gain_ref[...].astype(F32)
    mixed_grad = scale * (lifted - mixed_ref[0] * (scale * scale * inner))
    conv_grad = mixed_grad * staged_ref[1].astype(F32)
    grad_ref[...] = conv_grad.T.reshape(grad_ref.shape).astype(BF16)


def token_kernel(sums_ref, mixed_ref, staged_ref, gain_ref, normed_ref, residual_grad_ref, gate_grad_ref):
    scale, inner = token_scales(sums_ref)
    gain = gain_ref[...].astype(F32)
    mixed = mixed_ref[0]
    lifted = staged_ref[2].astype(F32) * gain
    normed_ref[...] = (mixed * scale * gain).astype(BF16)
    mixed_grad = scale * (lifted - mixed * (scale * scale * inner))
    residual_grad_ref[...] = mixed_grad.astype(BF16)
    gate_grad_ref[...] = (mixed_grad * mixed_ref[1]).astype(BF16)


def backward_kernel(spans_ref, slabs_ref, source_hbm, taps_hbm, table_ref, mixed_ref, out_ref, source_ref, taps_ref, up_ref, spec_ref, lag_ref, sems):
    kept = [
        pltpu.make_async_copy(source_hbm, source_ref, sems.at[0]),
        pltpu.make_async_copy(taps_hbm, taps_ref, sems.at[1]),
    ]
    for copy in kept:
        copy.start()
    signs = half_signs()
    up = to_spectrum(block_rows(slabs_ref[...].astype(F32)), table_ref)
    spec_ref[pl.ds(0, BLOCKS)] = up.reshape(BLOCKS, 8, SPEC)
    up_ref[...] = jnp.zeros((ROWS, 8, SPEC), F32)
    for doc in range(DOCS):
        start, end = doc_bounds(spans_ref, doc)

        @pl.loop(start, end)
        def _(n):
            up_ref[n + PAD * (doc + 1)] = spec_ref[n]

    for copy in kept:
        copy.wait()

    spec_ref[...] = jnp.zeros(spec_ref.shape, F32)
    for doc in range(DOCS):
        start, end = doc_bounds(spans_ref, doc)
        shift = PAD * (doc + 1)

        @pl.loop(0, tiles(end - start))
        def _(tile):
            first = start + TILE * tile

            def step(sums, k, count):
                rows = [first + TILE + k + shift + j for j in range(count)]
                return add_rows(sums, up_ref, rows, taps_ref, TILE + k + LAG_PAD, True)

            rows = [first + shift + j for j in range(TILE)]
            sums = add_rows(zero_sums(), up_ref, rows, taps_ref, LAG_PAD, True, triangle=True)
            store_tile(spec_ref, first, add_range(sums, end - first - TILE, step))

    lag_ref[pl.ds(BLOCKS, 1)] = jnp.zeros((1, 8, SPEC), F32)

    @pl.loop(0, BLOCKS // TILE)
    def _(tile):
        first = TILE * tile
        sums = zero_sums()
        for doc in range(DOCS):
            start, end = doc_bounds(spans_ref, doc)
            begin = start + PAD * (doc + 1)

            def step(sums, k, count):
                rows = [begin + first + TILE + k + j for j in range(count)]
                return add_rows(sums, up_ref, rows, source_ref, begin + TILE + k, True)

            def whole(_, sums):
                rows = [begin + first + j for j in range(TILE)]
                sums = add_rows(sums, up_ref, rows, source_ref, begin, True, triangle=True)
                return add_range(sums, end - start - first - TILE, step)

            sums = lax.fori_loop(0, (end - start > first).astype(jnp.int32), whole, sums)
        store_tile(lag_ref, first, sums)

    source_grad = from_spectrum(spec_ref[pl.ds(0, BLOCKS)].reshape(BLOCKS * 8, SPEC), table_ref)
    lags, later = lag_ref[pl.ds(0, BLOCKS)], lag_ref[pl.ds(1, BLOCKS)]
    folded = jnp.concatenate(
        [
            lags[..., :FREQS] + signs * later[..., FREQS:],
            lags[..., FREQS:] - signs * later[..., :FREQS],
        ],
        axis=2,
    )
    tap_grad = from_spectrum(folded.reshape(BLOCKS * 8, SPEC), table_ref)
    out_ref[...] = jnp.concatenate(
        [
            sender_slabs(source_grad * (1.0 / BLOCK), 8),
            sender_slabs(tap_grad * (TOKENS**-0.5 / BLOCK), 8),
        ],
        axis=1,
    ).astype(BF16)


def product_kernel(slabs_ref, values_ref, gate_ref, gate_grad_hbm, values_grad_hbm, filter_grad_hbm, gate_grad_ref, values_grad_ref, filter_grad_ref, sems):
    tokens, width = values_ref.shape
    part = tokens // 2
    leaving = []
    for k in range(2):
        rows = pl.ds(k * part, part)
        slabs = slabs_ref[:, :, rows].astype(F32)
        gated_grad = slabs[:, :8].reshape(width, part).T
        filter_grad_ref[rows] = slabs[:, 8:].reshape(width, part).T
        gate_grad_ref[rows] = (gated_grad * values_ref[rows].astype(F32)).astype(BF16)
        values_grad_ref[rows] = (gated_grad * gate_ref[rows].astype(F32)).astype(BF16)
        for which, (ref, hbm) in enumerate(
            (
                (filter_grad_ref, filter_grad_hbm),
                (gate_grad_ref, gate_grad_hbm),
                (values_grad_ref, values_grad_hbm),
            )
        ):
            leaving.append(pltpu.make_async_copy(ref.at[rows], hbm.at[rows], sems.at[which, k]))
            leaving[-1].start()
    for copy in leaving:
        copy.wait()


def call(kernel, ins, outs, scratch=(), limit=24, cost=4_000_000):
    spaces = {"v": pltpu.VMEM, "h": pltpu.HBM, "s": pltpu.SMEM}
    spec = lambda space: pl.BlockSpec(memory_space=spaces[space])
    return pl.pallas_call(
        kernel,
        out_shape=[
            pltpu.HBM(*shape) if space == "h" else jax.ShapeDtypeStruct(*shape)
            for shape, space in outs
        ],
        in_specs=[spec(space) for space in ins],
        out_specs=[spec(space) for _, space in outs],
        scratch_shapes=list(scratch),
        compiler_params=pltpu.CompilerParams(vmem_limit_bytes=limit * 1024 * 1024),
        cost_estimate=pl.CostEstimate(flops=cost, bytes_accessed=cost, transcendentals=0),
    )


def in_hbm(*arrays):
    return [pltpu.with_memory_space_constraint(array, pltpu.HBM) for array in arrays]


def exchange(array, axis):
    return lax.all_to_all(array, axis, split_axis=0, concat_axis=0, tiled=True)


SOURCE = ((ROWS, 8, SPEC), F32)
LAGS = ((LAG_ROWS, 8, SPEC), F32)
SUMS = ((PAD + BLOCKS, 8, SPEC), F32)


def vmem(shape):
    return pltpu.VMEM(*shape)


def run_forward(spans, slabs, table):
    single = ((slabs.shape[0], 8, slabs.shape[2]), BF16)
    return call(
        forward_kernel,
        "svv",
        [(single, "v"), (SOURCE, "h"), (LAGS, "h")],
        [vmem(SOURCE), vmem(LAGS), vmem(SUMS), pltpu.SemaphoreType.DMA((2,))],
    )(spans, slabs, table)


def run_backward(spans, slabs, source, taps, table, mixed):
    pair = ((slabs.shape[0], 16, slabs.shape[2]), BF16)
    return call(
        backward_kernel,
        "svhhvv",
        [(pair, "v")],
        [vmem(SOURCE), vmem(LAGS), vmem(SOURCE), vmem(SUMS), vmem(SUMS), pltpu.SemaphoreType.DMA((2,))],
    )(spans, slabs, *in_hbm(source, taps), table, mixed)[0]


def body(exchange, input_gate, output_gate, values, residual, cotangent, filters, gain, spans):
    tokens, width = input_gate.shape
    table = jnp.asarray(window_table())
    like, wide = ((tokens, width), BF16), ((tokens, width), F32)
    pair, single = ((64, 16, tokens), BF16), ((64, 8, tokens), BF16)
    sums_rows = ((8, 8, tokens), F32)
    dma = pltpu.SemaphoreType.DMA

    (outgoing,) = call(
        gate_kernel,
        "hhh",
        [(pair, "h")],
        [vmem(like), vmem(like), vmem(wide), vmem(pair), dma((3, CHUNKS)), dma((CHUNKS,))],
    )(*in_hbm(values, input_gate, filters))
    incoming = exchange(outgoing, "seq")
    (staged,) = call(stage_kernel, "hhh", [(((3, tokens, width), BF16), "v")], [dma((3,))])(
        *in_hbm(residual, output_gate, cotangent)
    )
    incoming, staged, gain = lax.optimization_barrier((incoming, staged, gain))
    conv, source, taps = run_forward(spans, incoming, table)
    conv = exchange(conv, "seq")
    mixed, sums = call(
        mixed_kernel, "vvv", [(((2, tokens, width), F32), "v"), (sums_rows, "v")]
    )(conv, staged, gain)
    sums = exchange(sums, "chan")
    (conv_grad,) = call(grad_kernel, "vvvv", [(single, "v")])(sums, mixed, staged, gain)
    conv_grad = exchange(conv_grad, "seq")
    normed, residual_grad, output_gate_grad = call(token_kernel, "vvvv", [(like, "v")] * 3)(
        sums, mixed, staged, gain
    )
    grads = run_backward(spans, conv_grad, source, taps, table, mixed)
    grads = exchange(grads, "seq")
    input_gate_grad, values_grad, filter_grad = call(
        product_kernel,
        "vvv",
        [(like, "h"), (like, "h"), (wide, "h")],
        [vmem(like), vmem(like), vmem(wide), dma((3, 2))],
    )(grads, values, input_gate)
    return (normed, residual_grad, input_gate_grad, output_gate_grad, values_grad, filter_grad)


def shards(input_gate, output_gate, values, residual, cotangent, filters, norm_gain, doc_spans):
    gain = norm_gain.reshape(1, norm_gain.shape[0])
    spans = doc_spans.reshape(2 * DOCS)
    return body(exchange, input_gate, output_gate, values, residual, cotangent, filters, gain, spans)


def solution(mesh):
    split = P("seq", "chan")
    return jax.shard_map(
        shards,
        mesh=mesh,
        in_specs=(split, split, split, split, split, split, P("chan"), P()),
        out_specs=(split,) * 6,
        check_vma=False,
    )
```

```python
import jax
import jax.numpy as jnp
import ml_dtypes
import numpy as np
from jax import lax
from jax.experimental import pallas as pl
from jax.experimental.pallas import tpu as pltpu
from jax.sharding import PartitionSpec as P

D = 4096
BLOCK = 512
TOKENS = 16384
DOCS = 4
EPSILON = 1e-06
BLOCKS = TOKENS // BLOCK
FREQS = BLOCK
SPEC = 2 * FREQS
TILE = 4
PAD = TILE
ROWS = BLOCKS + PAD * (DOCS + 2)
LAG_PAD = TILE
LAG_ROWS = LAG_PAD + BLOCKS
F32 = jnp.float32
BF16 = jnp.bfloat16


def window_table():
    places = np.arange(BLOCK, dtype=np.int64)
    odd = 2 * np.arange(FREQS, dtype=np.int64) + 1
    phase = (places[:, None] * odd[None, :] % (4 * BLOCK)) * (np.pi / (2 * BLOCK))
    forward = np.concatenate([np.cos(phase), -np.sin(phase)], axis=1) / 8
    high = forward.astype(ml_dtypes.bfloat16)
    low = (forward - high.astype(np.float64)).astype(ml_dtypes.bfloat16)
    return np.concatenate([high, low])


def half_signs():
    lanes = lax.broadcasted_iota(jnp.int32, (1, 1, FREQS), 2)
    return (1 - 2 * (lanes % 2)).astype(F32)


def block_rows(slabs):
    count, chans, width = slabs.shape
    pairs = slabs.reshape(count // 2, 2, chans, width)
    joined = jnp.concatenate([pairs[:, 0], pairs[:, 1]], axis=2)
    return joined.reshape(count // 2 * chans, 2 * width)


def sender_slabs(rows, chans):
    width = rows.shape[1] // 2
    blocks = rows.reshape(rows.shape[0] // chans, 1, chans, 2 * width)
    joined = jnp.concatenate([blocks[..., :width], blocks[..., width:]], axis=1)
    return joined.reshape(2 * blocks.shape[0], chans, width)


def to_spectrum(rows, table_ref):
    rows = rows.astype(BF16)
    return jnp.dot(jnp.concatenate([rows, rows], axis=1), table_ref[...], preferred_element_type=F32)


def from_spectrum(spec, table_ref):
    high = spec.astype(BF16)
    low = (spec - high.astype(F32)).astype(BF16)
    table = table_ref[pl.ds(0, BLOCK)]
    across = (((1,), (1,)), ((), ()))
    total = lax.dot_general(high, table, across, preferred_element_type=F32)
    return total + lax.dot_general(low, table, across, preferred_element_type=F32)


def doc_bounds(spans_ref, doc):
    return spans_ref[2 * doc] // BLOCK, spans_ref[2 * doc + 1] // BLOCK


COLUMNS = range(0, FREQS, 128)


def load_tile(ref, row):
    return tuple(
        tuple(
            (ref[row + i, :, pl.ds(lane, 128)], ref[row + i, :, pl.ds(FREQS + lane, 128)])
            for i in range(TILE)
        )
        for lane in COLUMNS
    )


def store_tile(ref, row, sums):
    for lane, column in zip(COLUMNS, sums):
        for i, (real, imag) in enumerate(column):
            ref[row + i, :, pl.ds(lane, 128)] = real
            ref[row + i, :, pl.ds(FREQS + lane, 128)] = imag


def zero_sums():
    zero = jnp.zeros((8, 128), F32)
    return tuple(tuple((zero, zero) for _ in range(TILE)) for _ in COLUMNS)


def add_rows(sums, rows_ref, rows, taps_ref, tap, conj, triangle=False):
    out = []
    for lane, column in zip(COLUMNS, sums):
        re_lanes, im_lanes = pl.ds(lane, 128), pl.ds(FREQS + lane, 128)
        column, seen = list(column), {}
        for j, row in enumerate(rows):
            a, b = rows_ref[row, :, re_lanes], rows_ref[row, :, im_lanes]
            for i in range(TILE):
                offset = j - i if conj else i - j
                if triangle and offset < 0:
                    continue
                if offset not in seen:
                    seen[offset] = (taps_ref[tap + offset, :, re_lanes], taps_ref[tap + offset, :, im_lanes])
                c, d = seen[offset]
                real, imag = column[i]
                if conj:
                    column[i] = (real + (c * a + d * b), imag + (c * b - d * a))
                else:
                    column[i] = (real + (c * a - d * b), imag + (c * b + d * a))
        out.append(tuple(column))
    return tuple(out)


def add_range(sums, count, step):
    count = jnp.maximum(count, 0)
    full = count // TILE
    sums = lax.fori_loop(0, full, lambda g, sums: step(sums, TILE * g, TILE), sums)
    return lax.fori_loop(TILE * full, count, lambda k, sums: step(sums, k, 1), sums)


def zero_gaps(spans_ref, ref, shift):
    for doc in range(DOCS - 1):
        _, end = doc_bounds(spans_ref, doc)
        start, _ = doc_bounds(spans_ref, doc + 1)

        @pl.loop(end, start)
        def _(n):
            ref[n + shift] = jnp.zeros(ref.shape[1:], F32)


def tiles(length):
    return (length + TILE - 1) // TILE


CHUNKS = 4


def gate_kernel(values_hbm, gate_hbm, filters_hbm, out_hbm, values_ref, gate_ref, filters_ref, out_ref, sems, out_sems):
    width = values_ref.shape[1] // CHUNKS
    slabs, twice, tokens = out_ref.shape
    slabs //= CHUNKS
    shape = (slabs, twice // 2, tokens)
    arriving = []
    for chunk in range(CHUNKS):
        lanes = pl.ds(chunk * width, width)
        arriving.append(
            [
                pltpu.make_async_copy(hbm.at[:, lanes], ref.at[:, lanes], sems.at[k, chunk])
                for k, (hbm, ref) in enumerate(
                    ((values_hbm, values_ref), (gate_hbm, gate_ref), (filters_hbm, filters_ref))
                )
            ]
        )
        for copy in arriving[-1]:
            copy.start()
    leaving = []
    for chunk in range(CHUNKS):
        lanes, rows = pl.ds(chunk * width, width), pl.ds(chunk * slabs, slabs)
        for copy in arriving[chunk]:
            copy.wait()
        gated = values_ref[:, lanes].astype(F32) * gate_ref[:, lanes].astype(F32)
        both = jnp.concatenate(
            [gated.T.reshape(shape), filters_ref[:, lanes].T.reshape(shape)], axis=1
        )
        out_ref[rows] = both.astype(BF16)
        leaving.append(pltpu.make_async_copy(out_ref.at[rows], out_hbm.at[rows], out_sems.at[chunk]))
        leaving[-1].start()
    for copy in leaving:
        copy.wait()


def stage_kernel(residual_hbm, gate_hbm, cotangent_hbm, staged_ref, sems):
    copies = [
        pltpu.make_async_copy(hbm, staged_ref.at[k], sems.at[k])
        for k, hbm in enumerate((residual_hbm, gate_hbm, cotangent_hbm))
    ]
    for copy in copies:
        copy.start()
    for copy in copies:
        copy.wait()


def forward_kernel(spans_ref, slabs_ref, table_ref, conv_ref, source_ref, taps_ref, spec_ref):
    signs = half_signs()
    both = to_spectrum(block_rows(slabs_ref[...]), table_ref).reshape(BLOCKS, 16, SPEC)
    spec_ref[pl.ds(0, BLOCKS)] = both[:, :8]
    real, imag = both[:, 8:, :FREQS], both[:, 8:, FREQS:]
    nothing = jnp.zeros((1, 8, FREQS), F32)
    before_real = jnp.concatenate([nothing, real[:-1]], axis=0)
    before_imag = jnp.concatenate([nothing, imag[:-1]], axis=0)
    taps_ref[pl.ds(0, LAG_PAD)] = jnp.zeros((LAG_PAD, 8, SPEC), F32)
    taps_ref[pl.ds(LAG_PAD, BLOCKS), :, :FREQS] = real - signs * before_imag
    taps_ref[pl.ds(LAG_PAD, BLOCKS), :, FREQS:] = imag + signs * before_real
    source_ref[...] = jnp.zeros((ROWS, 8, SPEC), F32)
    for doc in range(DOCS):
        start, end = doc_bounds(spans_ref, doc)

        @pl.loop(start, end)
        def _(n):
            source_ref[n + PAD * (doc + 1)] = spec_ref[n]

    zero_gaps(spans_ref, spec_ref, PAD)
    for doc in reversed(range(DOCS)):
        start, end = doc_bounds(spans_ref, doc)
        shift = PAD * (doc + 1)

        @pl.loop(0, tiles(end - start))
        def _(tile):
            first = end - TILE * (tile + 1)

            def step(sums, k, count):
                s = first - k - count
                rows = [s + shift + j for j in range(count)]
                return add_rows(sums, source_ref, rows, taps_ref, first - s + LAG_PAD, False)

            rows = [first + shift + j for j in range(TILE)]
            sums = add_rows(zero_sums(), source_ref, rows, taps_ref, LAG_PAD, False, triangle=True)
            store_tile(spec_ref, first + PAD, add_range(sums, first - start, step))

    total = spec_ref[pl.ds(PAD, BLOCKS)].reshape(BLOCKS * 8, SPEC)
    conv = from_spectrum(total, table_ref)
    conv_ref[...] = sender_slabs(conv, 8).astype(BF16)


def mixed_kernel(conv_ref, staged_ref, gain_ref, source_ref, taps_ref, mixed_ref, sums_ref):
    _, tokens, width = staged_ref.shape
    conv = conv_ref[...].astype(F32).reshape(width, tokens).T
    mixed = staged_ref[0].astype(F32) + conv * staged_ref[1].astype(F32)
    lifted = staged_ref[2].astype(F32) * gain_ref[...].astype(F32)
    mixed_ref[0] = mixed
    mixed_ref[1] = conv
    power = jnp.sum(mixed * mixed, axis=1, keepdims=True)
    inner = jnp.sum(lifted * mixed, axis=1, keepdims=True)
    lanes = lax.broadcasted_iota(jnp.int32, (tokens, 128), 1)
    both = jnp.where(lanes == 0, power, jnp.where(lanes == 1, inner, 0.0)).T[:8]
    sums_ref[...] = jnp.broadcast_to(both[None], sums_ref.shape)


def token_scales(sums_ref):
    total = jnp.sum(sums_ref[...], axis=0)
    padded = jnp.concatenate([total, jnp.zeros((120, total.shape[1]), F32)], axis=0).T
    scale = lax.rsqrt(padded[:, 0:1] / D + EPSILON)
    return scale, padded[:, 1:2] / D


def grad_kernel(sums_ref, mixed_ref, staged_ref, gain_ref, source_ref, taps_ref, grad_ref):
    scale, inner = token_scales(sums_ref)
    lifted = staged_ref[2].astype(F32) * gain_ref[...].astype(F32)
    mixed_grad = scale * (lifted - mixed_ref[0] * (scale * scale * inner))
    conv_grad = mixed_grad * staged_ref[1].astype(F32)
    grad_ref[...] = conv_grad.T.reshape(grad_ref.shape).astype(BF16)


def token_kernel(sums_ref, mixed_ref, staged_ref, gain_ref, normed_ref, residual_grad_ref, gate_grad_ref):
    scale, inner = token_scales(sums_ref)
    gain = gain_ref[...].astype(F32)
    mixed = mixed_ref[0]
    lifted = staged_ref[2].astype(F32) * gain
    normed_ref[...] = (mixed * scale * gain).astype(BF16)
    mixed_grad = scale * (lifted - mixed * (scale * scale * inner))
    residual_grad_ref[...] = mixed_grad.astype(BF16)
    gate_grad_ref[...] = (mixed_grad * mixed_ref[1]).astype(BF16)


def backward_kernel(spans_ref, slabs_ref, source_ref, taps_ref, table_ref, mixed_ref, out_ref, up_ref, spec_ref, lag_ref):
    signs = half_signs()
    up = to_spectrum(block_rows(slabs_ref[...].astype(F32)), table_ref)
    spec_ref[pl.ds(0, BLOCKS)] = up.reshape(BLOCKS, 8, SPEC)
    up_ref[...] = jnp.zeros((ROWS, 8, SPEC), F32)
    for doc in range(DOCS):
        start, end = doc_bounds(spans_ref, doc)

        @pl.loop(start, end)
        def _(n):
            up_ref[n + PAD * (doc + 1)] = spec_ref[n]

    zero_gaps(spans_ref, spec_ref, 0)
    for doc in range(DOCS):
        start, end = doc_bounds(spans_ref, doc)
        shift = PAD * (doc + 1)

        @pl.loop(0, tiles(end - start))
        def _(tile):
            first = start + TILE * tile

            def step(sums, k, count):
                rows = [first + TILE + k + shift + j for j in range(count)]
                return add_rows(sums, up_ref, rows, taps_ref, TILE + k + LAG_PAD, True)

            rows = [first + shift + j for j in range(TILE)]
            sums = add_rows(zero_sums(), up_ref, rows, taps_ref, LAG_PAD, True, triangle=True)
            store_tile(spec_ref, first, add_range(sums, end - first - TILE, step))

    lag_ref[...] = jnp.zeros(lag_ref.shape, F32)
    for doc in range(DOCS):
        start, end = doc_bounds(spans_ref, doc)
        begin = start + PAD * (doc + 1)

        @pl.loop(0, tiles(end - start))
        def _(tile):
            first = TILE * tile

            def step(sums, k, count):
                rows = [begin + first + TILE + k + j for j in range(count)]
                return add_rows(sums, up_ref, rows, source_ref, begin + TILE + k, True)

            rows = [begin + first + j for j in range(TILE)]
            sums = add_rows(load_tile(lag_ref, first), up_ref, rows, source_ref, begin, True, triangle=True)
            store_tile(lag_ref, first, add_range(sums, end - start - first - TILE, step))

    source_grad = from_spectrum(spec_ref[pl.ds(0, BLOCKS)].reshape(BLOCKS * 8, SPEC), table_ref)
    lags, later = lag_ref[pl.ds(0, BLOCKS)], lag_ref[pl.ds(1, BLOCKS)]
    folded = jnp.concatenate(
        [
            lags[..., :FREQS] + signs * later[..., FREQS:],
            lags[..., FREQS:] - signs * later[..., :FREQS],
        ],
        axis=2,
    )
    tap_grad = from_spectrum(folded.reshape(BLOCKS * 8, SPEC), table_ref)
    out_ref[...] = jnp.concatenate(
        [
            sender_slabs(source_grad, 8),
            sender_slabs(tap_grad * TOKENS**-0.5, 8),
        ],
        axis=1,
    ).astype(BF16)


def product_kernel(slabs_ref, values_ref, gate_ref, gate_grad_hbm, values_grad_hbm, filter_grad_hbm, gate_grad_ref, values_grad_ref, filter_grad_ref, sems):
    tokens, width = values_ref.shape
    part = tokens // 2
    leaving = []
    for k in range(2):
        rows = pl.ds(k * part, part)
        slabs = slabs_ref[:, :, rows].astype(F32)
        gated_grad = slabs[:, :8].reshape(width, part).T
        filter_grad_ref[rows] = slabs[:, 8:].reshape(width, part).T
        gate_grad_ref[rows] = (gated_grad * values_ref[rows].astype(F32)).astype(BF16)
        values_grad_ref[rows] = (gated_grad * gate_ref[rows].astype(F32)).astype(BF16)
        for which, (ref, hbm) in enumerate(
            (
                (filter_grad_ref, filter_grad_hbm),
                (gate_grad_ref, gate_grad_hbm),
                (values_grad_ref, values_grad_hbm),
            )
        ):
            leaving.append(pltpu.make_async_copy(ref.at[rows], hbm.at[rows], sems.at[which, k]))
            leaving[-1].start()
    for copy in leaving:
        copy.wait()


def call(kernel, ins, outs, scratch=(), limit=24, cost=4_000_000):
    spaces = {"v": pltpu.VMEM, "h": pltpu.HBM, "s": pltpu.SMEM}
    spec = lambda space: pl.BlockSpec(memory_space=spaces[space])
    return pl.pallas_call(
        kernel,
        out_shape=[
            pltpu.HBM(*shape) if space == "h" else jax.ShapeDtypeStruct(*shape)
            for shape, space in outs
        ],
        in_specs=[spec(space) for space in ins],
        out_specs=[spec(space) for _, space in outs],
        scratch_shapes=list(scratch),
        compiler_params=pltpu.CompilerParams(vmem_limit_bytes=limit * 1024 * 1024),
        cost_estimate=pl.CostEstimate(flops=cost, bytes_accessed=cost, transcendentals=0),
    )


def in_hbm(*arrays):
    return [pltpu.with_memory_space_constraint(array, pltpu.HBM) for array in arrays]


def exchange(array, axis):
    return lax.all_to_all(array, axis, split_axis=0, concat_axis=0, tiled=True)


SOURCE = ((ROWS, 8, SPEC), F32)
LAGS = ((LAG_ROWS, 8, SPEC), F32)
SUMS = ((PAD + BLOCKS, 8, SPEC), F32)


def vmem(shape):
    return pltpu.VMEM(*shape)


def run_forward(spans, slabs, table):
    single = ((slabs.shape[0], 8, slabs.shape[2]), BF16)
    return call(
        forward_kernel,
        "svv",
        [(single, "v"), (SOURCE, "v"), (LAGS, "v")],
        [vmem(SUMS)],
    )(spans, slabs, table)


def run_backward(spans, slabs, source, taps, table, mixed):
    pair = ((slabs.shape[0], 16, slabs.shape[2]), BF16)
    return call(
        backward_kernel,
        "svvvvv",
        [(pair, "v")],
        [vmem(SOURCE), vmem(SUMS), vmem(SUMS)],
    )(spans, slabs, source, taps, table, mixed)[0]


def body(exchange, input_gate, output_gate, values, residual, cotangent, filters, gain, spans):
    tokens, width = input_gate.shape
    table = jnp.asarray(window_table())
    like, wide = ((tokens, width), BF16), ((tokens, width), F32)
    pair, single = ((64, 16, tokens), BF16), ((64, 8, tokens), BF16)
    sums_rows = ((8, 8, tokens), F32)
    dma = pltpu.SemaphoreType.DMA

    (outgoing,) = call(
        gate_kernel,
        "hhh",
        [(pair, "h")],
        [vmem(like), vmem(like), vmem(wide), vmem(pair), dma((3, CHUNKS)), dma((CHUNKS,))],
    )(*in_hbm(values, input_gate, filters))
    incoming = exchange(outgoing, "seq")
    (staged,) = call(stage_kernel, "hhh", [(((3, tokens, width), BF16), "v")], [dma((3,))])(
        *in_hbm(residual, output_gate, cotangent)
    )
    incoming, staged, gain = lax.optimization_barrier((incoming, staged, gain))
    conv, source, taps = run_forward(spans, incoming, table)
    conv = exchange(conv, "seq")
    mixed, sums = call(
        mixed_kernel, "vvvvv", [(((2, tokens, width), F32), "v"), (sums_rows, "v")]
    )(conv, staged, gain, source, taps)
    sums = exchange(sums, "chan")
    (conv_grad,) = call(grad_kernel, "vvvvvv", [(single, "v")])(sums, mixed, staged, gain, source, taps)
    conv_grad = exchange(conv_grad, "seq")
    normed, residual_grad, output_gate_grad = call(token_kernel, "vvvv", [(like, "v")] * 3)(
        sums, mixed, staged, gain
    )
    grads = run_backward(spans, conv_grad, source, taps, table, mixed)
    grads = exchange(grads, "seq")
    input_gate_grad, values_grad, filter_grad = call(
        product_kernel,
        "vvv",
        [(like, "h"), (like, "h"), (wide, "h")],
        [vmem(like), vmem(like), vmem(wide), dma((3, 2))],
    )(grads, values, input_gate)
    return (normed, residual_grad, input_gate_grad, output_gate_grad, values_grad, filter_grad)


def shards(input_gate, output_gate, values, residual, cotangent, filters, norm_gain, doc_spans):
    gain = norm_gain.reshape(1, norm_gain.shape[0])
    spans = doc_spans.reshape(2 * DOCS)
    return body(exchange, input_gate, output_gate, values, residual, cotangent, filters, gain, spans)


def solution(mesh):
    split = P("seq", "chan")
    return jax.shard_map(
        shards,
        mesh=mesh,
        in_specs=(split, split, split, split, split, split, P("chan"), P()),
        out_specs=(split,) * 6,
        check_vma=False,
    )
```

```python
import jax
import jax.numpy as jnp
import ml_dtypes
import numpy as np
from jax import lax
from jax.experimental import pallas as pl
from jax.experimental.pallas import tpu as pltpu
from jax.sharding import PartitionSpec as P

D = 4096
BLOCK = 512
TOKENS = 16384
DOCS = 4
EPSILON = 1e-06
BLOCKS = TOKENS // BLOCK
FREQS = BLOCK
SPEC = 2 * FREQS
TILE = 4
PAD = TILE
ROWS = BLOCKS + PAD * (DOCS + 2)
LAG_PAD = TILE
LAG_ROWS = LAG_PAD + BLOCKS
F32 = jnp.float32
BF16 = jnp.bfloat16


def window_table():
    places = np.arange(BLOCK, dtype=np.int64)
    odd = 2 * np.arange(FREQS, dtype=np.int64) + 1
    phase = (places[:, None] * odd[None, :] % (4 * BLOCK)) * (np.pi / (2 * BLOCK))
    forward = np.concatenate([np.cos(phase), -np.sin(phase)], axis=1) / 8
    high = forward.astype(ml_dtypes.bfloat16)
    low = (forward - high.astype(np.float64)).astype(ml_dtypes.bfloat16)
    return np.concatenate([high, low])


def half_signs():
    lanes = lax.broadcasted_iota(jnp.int32, (1, 1, FREQS), 2)
    return (1 - 2 * (lanes % 2)).astype(F32)


def block_rows(slabs):
    count, chans, width = slabs.shape
    pairs = slabs.reshape(count // 2, 2, chans, width)
    joined = jnp.concatenate([pairs[:, 0], pairs[:, 1]], axis=2)
    return joined.reshape(count // 2 * chans, 2 * width)


def sender_slabs(rows, chans):
    width = rows.shape[1] // 2
    blocks = rows.reshape(rows.shape[0] // chans, 1, chans, 2 * width)
    joined = jnp.concatenate([blocks[..., :width], blocks[..., width:]], axis=1)
    return joined.reshape(2 * blocks.shape[0], chans, width)


def to_spectrum(rows, table_ref):
    rows = rows.astype(BF16)
    return jnp.dot(jnp.concatenate([rows, rows], axis=1), table_ref[...], preferred_element_type=F32)


def from_spectrum(spec, table_ref):
    across = (((1,), (1,)), ((), ()))
    return lax.dot_general(spec.astype(BF16), table_ref[pl.ds(0, BLOCK)], across, preferred_element_type=F32)


def doc_bounds(spans_ref, doc):
    return spans_ref[2 * doc] // BLOCK, spans_ref[2 * doc + 1] // BLOCK


COLUMNS = range(0, FREQS, 128)


def load_tile(ref, row):
    return tuple(
        tuple(
            (ref[row + i, :, pl.ds(lane, 128)], ref[row + i, :, pl.ds(FREQS + lane, 128)])
            for i in range(TILE)
        )
        for lane in COLUMNS
    )


def store_tile(ref, row, sums):
    for lane, column in zip(COLUMNS, sums):
        for i, (real, imag) in enumerate(column):
            ref[row + i, :, pl.ds(lane, 128)] = real
            ref[row + i, :, pl.ds(FREQS + lane, 128)] = imag


def zero_sums():
    zero = jnp.zeros((8, 128), F32)
    return tuple(tuple((zero, zero) for _ in range(TILE)) for _ in COLUMNS)


def add_rows(sums, rows_ref, rows, taps_ref, tap, conj, triangle=False):
    out = []
    for lane, column in zip(COLUMNS, sums):
        re_lanes, im_lanes = pl.ds(lane, 128), pl.ds(FREQS + lane, 128)
        column, seen = list(column), {}
        for j, row in enumerate(rows):
            a, b = rows_ref[row, :, re_lanes], rows_ref[row, :, im_lanes]
            for i in range(TILE):
                offset = j - i if conj else i - j
                if triangle and offset < 0:
                    continue
                if offset not in seen:
                    seen[offset] = (taps_ref[tap + offset, :, re_lanes], taps_ref[tap + offset, :, im_lanes])
                c, d = seen[offset]
                real, imag = column[i]
                if conj:
                    column[i] = (real + (c * a + d * b), imag + (c * b - d * a))
                else:
                    column[i] = (real + (c * a - d * b), imag + (c * b + d * a))
        out.append(tuple(column))
    return tuple(out)


def add_range(sums, count, step):
    count = jnp.maximum(count, 0)
    full = count // TILE
    sums = lax.fori_loop(0, full, lambda g, sums: step(sums, TILE * g, TILE), sums)
    return lax.fori_loop(TILE * full, count, lambda k, sums: step(sums, k, 1), sums)


def zero_gaps(spans_ref, ref, shift):
    for doc in range(DOCS - 1):
        _, end = doc_bounds(spans_ref, doc)
        start, _ = doc_bounds(spans_ref, doc + 1)

        @pl.loop(end, start)
        def _(n):
            ref[n + shift] = jnp.zeros(ref.shape[1:], F32)


def tiles(length):
    return (length + TILE - 1) // TILE


CHUNKS = 4


def gate_kernel(values_hbm, gate_hbm, filters_hbm, out_hbm, values_ref, gate_ref, filters_ref, out_ref, sems, out_sems):
    width = values_ref.shape[1] // CHUNKS
    slabs, twice, tokens = out_ref.shape
    slabs //= CHUNKS
    shape = (slabs, twice // 2, tokens)
    arriving = []
    for chunk in range(CHUNKS):
        lanes = pl.ds(chunk * width, width)
        arriving.append(
            [
                pltpu.make_async_copy(hbm.at[:, lanes], ref.at[:, lanes], sems.at[k, chunk])
                for k, (hbm, ref) in enumerate(
                    ((values_hbm, values_ref), (gate_hbm, gate_ref), (filters_hbm, filters_ref))
                )
            ]
        )
        for copy in arriving[-1]:
            copy.start()
    leaving = []
    for chunk in range(CHUNKS):
        lanes, rows = pl.ds(chunk * width, width), pl.ds(chunk * slabs, slabs)
        for copy in arriving[chunk]:
            copy.wait()
        gated = values_ref[:, lanes].astype(F32) * gate_ref[:, lanes].astype(F32)
        both = jnp.concatenate(
            [gated.T.reshape(shape), filters_ref[:, lanes].T.reshape(shape)], axis=1
        )
        out_ref[rows] = both.astype(BF16)
        leaving.append(pltpu.make_async_copy(out_ref.at[rows], out_hbm.at[rows], out_sems.at[chunk]))
        leaving[-1].start()
    for copy in leaving:
        copy.wait()


def stage_kernel(residual_hbm, gate_hbm, cotangent_hbm, staged_ref, sems):
    copies = [
        pltpu.make_async_copy(hbm, staged_ref.at[k], sems.at[k])
        for k, hbm in enumerate((residual_hbm, gate_hbm, cotangent_hbm))
    ]
    for copy in copies:
        copy.start()
    for copy in copies:
        copy.wait()


def forward_kernel(spans_ref, slabs_ref, table_ref, conv_ref, source_ref, taps_ref, spec_ref):
    signs = half_signs()
    both = to_spectrum(block_rows(slabs_ref[...]), table_ref).reshape(BLOCKS, 16, SPEC)
    spec_ref[pl.ds(0, BLOCKS)] = both[:, :8]
    real, imag = both[:, 8:, :FREQS], both[:, 8:, FREQS:]
    nothing = jnp.zeros((1, 8, FREQS), F32)
    before_real = jnp.concatenate([nothing, real[:-1]], axis=0)
    before_imag = jnp.concatenate([nothing, imag[:-1]], axis=0)
    taps_ref[pl.ds(0, LAG_PAD)] = jnp.zeros((LAG_PAD, 8, SPEC), F32)
    taps_ref[pl.ds(LAG_PAD, BLOCKS), :, :FREQS] = real - signs * before_imag
    taps_ref[pl.ds(LAG_PAD, BLOCKS), :, FREQS:] = imag + signs * before_real
    source_ref[...] = jnp.zeros((ROWS, 8, SPEC), F32)
    for doc in range(DOCS):
        start, end = doc_bounds(spans_ref, doc)

        @pl.loop(start, end)
        def _(n):
            source_ref[n + PAD * (doc + 1)] = spec_ref[n]

    zero_gaps(spans_ref, spec_ref, PAD)
    for doc in reversed(range(DOCS)):
        start, end = doc_bounds(spans_ref, doc)
        shift = PAD * (doc + 1)

        @pl.loop(0, tiles(end - start))
        def _(tile):
            first = end - TILE * (tile + 1)

            def step(sums, k, count):
                s = first - k - count
                rows = [s + shift + j for j in range(count)]
                return add_rows(sums, source_ref, rows, taps_ref, first - s + LAG_PAD, False)

            rows = [first + shift + j for j in range(TILE)]
            sums = add_rows(zero_sums(), source_ref, rows, taps_ref, LAG_PAD, False, triangle=True)
            store_tile(spec_ref, first + PAD, add_range(sums, first - start, step))

    total = spec_ref[pl.ds(PAD, BLOCKS)].reshape(BLOCKS * 8, SPEC)
    conv = from_spectrum(total, table_ref)
    conv_ref[...] = sender_slabs(conv, 8).astype(BF16)


def mixed_kernel(conv_ref, staged_ref, gain_ref, source_ref, taps_ref, mixed_ref, sums_ref):
    _, tokens, width = staged_ref.shape
    conv = conv_ref[...].astype(F32).reshape(width, tokens).T
    mixed = staged_ref[0].astype(F32) + conv * staged_ref[1].astype(F32)
    lifted = staged_ref[2].astype(F32) * gain_ref[...].astype(F32)
    mixed_ref[0] = mixed
    mixed_ref[1] = conv
    power = jnp.sum(mixed * mixed, axis=1, keepdims=True)
    inner = jnp.sum(lifted * mixed, axis=1, keepdims=True)
    lanes = lax.broadcasted_iota(jnp.int32, (tokens, 128), 1)
    both = jnp.where(lanes == 0, power, jnp.where(lanes == 1, inner, 0.0)).T[:8]
    sums_ref[...] = jnp.broadcast_to(both[None], sums_ref.shape)


def token_scales(sums_ref):
    total = jnp.sum(sums_ref[...], axis=0)
    padded = jnp.concatenate([total, jnp.zeros((120, total.shape[1]), F32)], axis=0).T
    scale = lax.rsqrt(padded[:, 0:1] / D + EPSILON)
    return scale, padded[:, 1:2] / D


def grad_kernel(sums_ref, mixed_ref, staged_ref, gain_ref, source_ref, taps_ref, grad_ref):
    scale, inner = token_scales(sums_ref)
    lifted = staged_ref[2].astype(F32) * gain_ref[...].astype(F32)
    mixed_grad = scale * (lifted - mixed_ref[0] * (scale * scale * inner))
    conv_grad = mixed_grad * staged_ref[1].astype(F32)
    grad_ref[...] = conv_grad.T.reshape(grad_ref.shape).astype(BF16)


def token_kernel(sums_ref, mixed_ref, staged_ref, gain_ref, normed_ref, residual_grad_ref, gate_grad_ref):
    scale, inner = token_scales(sums_ref)
    gain = gain_ref[...].astype(F32)
    mixed = mixed_ref[0]
    lifted = staged_ref[2].astype(F32) * gain
    normed_ref[...] = (mixed * scale * gain).astype(BF16)
    mixed_grad = scale * (lifted - mixed * (scale * scale * inner))
    residual_grad_ref[...] = mixed_grad.astype(BF16)
    gate_grad_ref[...] = (mixed_grad * mixed_ref[1]).astype(BF16)


def backward_kernel(spans_ref, slabs_ref, source_ref, taps_ref, table_ref, mixed_ref, out_ref, up_ref, spec_ref, lag_ref):
    signs = half_signs()
    up = to_spectrum(block_rows(slabs_ref[...].astype(F32)), table_ref)
    spec_ref[pl.ds(0, BLOCKS)] = up.reshape(BLOCKS, 8, SPEC)
    up_ref[...] = jnp.zeros((ROWS, 8, SPEC), F32)
    for doc in range(DOCS):
        start, end = doc_bounds(spans_ref, doc)

        @pl.loop(start, end)
        def _(n):
            up_ref[n + PAD * (doc + 1)] = spec_ref[n]

    zero_gaps(spans_ref, spec_ref, 0)
    for doc in range(DOCS):
        start, end = doc_bounds(spans_ref, doc)
        shift = PAD * (doc + 1)

        @pl.loop(0, tiles(end - start))
        def _(tile):
            first = start + TILE * tile

            def step(sums, k, count):
                rows = [first + TILE + k + shift + j for j in range(count)]
                return add_rows(sums, up_ref, rows, taps_ref, TILE + k + LAG_PAD, True)

            rows = [first + shift + j for j in range(TILE)]
            sums = add_rows(zero_sums(), up_ref, rows, taps_ref, LAG_PAD, True, triangle=True)
            store_tile(spec_ref, first, add_range(sums, end - first - TILE, step))

    lag_ref[...] = jnp.zeros(lag_ref.shape, F32)
    for doc in range(DOCS):
        start, end = doc_bounds(spans_ref, doc)
        begin = start + PAD * (doc + 1)

        @pl.loop(0, tiles(end - start))
        def _(tile):
            first = TILE * tile

            def step(sums, k, count):
                rows = [begin + first + TILE + k + j for j in range(count)]
                return add_rows(sums, up_ref, rows, source_ref, begin + TILE + k, True)

            rows = [begin + first + j for j in range(TILE)]
            sums = add_rows(load_tile(lag_ref, first), up_ref, rows, source_ref, begin, True, triangle=True)
            store_tile(lag_ref, first, add_range(sums, end - start - first - TILE, step))

    source_grad = from_spectrum(spec_ref[pl.ds(0, BLOCKS)].reshape(BLOCKS * 8, SPEC), table_ref)
    lags, later = lag_ref[pl.ds(0, BLOCKS)], lag_ref[pl.ds(1, BLOCKS)]
    folded = jnp.concatenate(
        [
            lags[..., :FREQS] + signs * later[..., FREQS:],
            lags[..., FREQS:] - signs * later[..., :FREQS],
        ],
        axis=2,
    )
    tap_grad = from_spectrum(folded.reshape(BLOCKS * 8, SPEC), table_ref)
    out_ref[...] = jnp.concatenate(
        [
            sender_slabs(source_grad, 8),
            sender_slabs(tap_grad * TOKENS**-0.5, 8),
        ],
        axis=1,
    ).astype(BF16)


def product_kernel(slabs_ref, values_ref, gate_ref, gate_grad_hbm, values_grad_hbm, filter_grad_hbm, gate_grad_ref, values_grad_ref, filter_grad_ref, sems):
    tokens, width = values_ref.shape
    part = tokens // 2
    leaving = []
    for k in range(2):
        rows = pl.ds(k * part, part)
        slabs = slabs_ref[:, :, rows].astype(F32)
        gated_grad = slabs[:, :8].reshape(width, part).T
        filter_grad_ref[rows] = slabs[:, 8:].reshape(width, part).T
        gate_grad_ref[rows] = (gated_grad * values_ref[rows].astype(F32)).astype(BF16)
        values_grad_ref[rows] = (gated_grad * gate_ref[rows].astype(F32)).astype(BF16)
        for which, (ref, hbm) in enumerate(
            (
                (filter_grad_ref, filter_grad_hbm),
                (gate_grad_ref, gate_grad_hbm),
                (values_grad_ref, values_grad_hbm),
            )
        ):
            leaving.append(pltpu.make_async_copy(ref.at[rows], hbm.at[rows], sems.at[which, k]))
            leaving[-1].start()
    for copy in leaving:
        copy.wait()


def call(kernel, ins, outs, scratch=(), limit=24, cost=4_000_000):
    spaces = {"v": pltpu.VMEM, "h": pltpu.HBM, "s": pltpu.SMEM}
    spec = lambda space: pl.BlockSpec(memory_space=spaces[space])
    return pl.pallas_call(
        kernel,
        out_shape=[
            pltpu.HBM(*shape) if space == "h" else jax.ShapeDtypeStruct(*shape)
            for shape, space in outs
        ],
        in_specs=[spec(space) for space in ins],
        out_specs=[spec(space) for _, space in outs],
        scratch_shapes=list(scratch),
        compiler_params=pltpu.CompilerParams(vmem_limit_bytes=limit * 1024 * 1024),
        cost_estimate=pl.CostEstimate(flops=cost, bytes_accessed=cost, transcendentals=0),
    )


def in_hbm(*arrays):
    return [pltpu.with_memory_space_constraint(array, pltpu.HBM) for array in arrays]


def exchange(array, axis):
    return lax.all_to_all(array, axis, split_axis=0, concat_axis=0, tiled=True)


SOURCE = ((ROWS, 8, SPEC), F32)
LAGS = ((LAG_ROWS, 8, SPEC), F32)
SUMS = ((PAD + BLOCKS, 8, SPEC), F32)


def vmem(shape):
    return pltpu.VMEM(*shape)


def run_forward(spans, slabs, table):
    single = ((slabs.shape[0], 8, slabs.shape[2]), BF16)
    return call(
        forward_kernel,
        "svv",
        [(single, "v"), (SOURCE, "v"), (LAGS, "v")],
        [vmem(SUMS)],
    )(spans, slabs, table)


def run_backward(spans, slabs, source, taps, table, mixed):
    pair = ((slabs.shape[0], 16, slabs.shape[2]), BF16)
    return call(
        backward_kernel,
        "svvvvv",
        [(pair, "v")],
        [vmem(SOURCE), vmem(SUMS), vmem(SUMS)],
    )(spans, slabs, source, taps, table, mixed)[0]


def body(exchange, input_gate, output_gate, values, residual, cotangent, filters, gain, spans):
    tokens, width = input_gate.shape
    table = jnp.asarray(window_table())
    like, wide = ((tokens, width), BF16), ((tokens, width), F32)
    pair, single = ((64, 16, tokens), BF16), ((64, 8, tokens), BF16)
    sums_rows = ((8, 8, tokens), F32)
    dma = pltpu.SemaphoreType.DMA

    (outgoing,) = call(
        gate_kernel,
        "hhh",
        [(pair, "h")],
        [vmem(like), vmem(like), vmem(wide), vmem(pair), dma((3, CHUNKS)), dma((CHUNKS,))],
    )(*in_hbm(values, input_gate, filters))
    incoming = exchange(outgoing, "seq")
    (staged,) = call(stage_kernel, "hhh", [(((3, tokens, width), BF16), "v")], [dma((3,))])(
        *in_hbm(residual, output_gate, cotangent)
    )
    incoming, staged, gain = lax.optimization_barrier((incoming, staged, gain))
    conv, source, taps = run_forward(spans, incoming, table)
    conv = exchange(conv, "seq")
    mixed, sums = call(
        mixed_kernel, "vvvvv", [(((2, tokens, width), F32), "v"), (sums_rows, "v")]
    )(conv, staged, gain, source, taps)
    sums = exchange(sums, "chan")
    (conv_grad,) = call(grad_kernel, "vvvvvv", [(single, "v")])(sums, mixed, staged, gain, source, taps)
    conv_grad = exchange(conv_grad, "seq")
    normed, residual_grad, output_gate_grad = call(token_kernel, "vvvv", [(like, "v")] * 3)(
        sums, mixed, staged, gain
    )
    grads = run_backward(spans, conv_grad, source, taps, table, mixed)
    grads = exchange(grads, "seq")
    input_gate_grad, values_grad, filter_grad = call(
        product_kernel,
        "vvv",
        [(like, "h"), (like, "h"), (wide, "h")],
        [vmem(like), vmem(like), vmem(wide), dma((3, 2))],
    )(grads, values, input_gate)
    return (normed, residual_grad, input_gate_grad, output_gate_grad, values_grad, filter_grad)


def shards(input_gate, output_gate, values, residual, cotangent, filters, norm_gain, doc_spans):
    gain = norm_gain.reshape(1, norm_gain.shape[0])
    spans = doc_spans.reshape(2 * DOCS)
    return body(exchange, input_gate, output_gate, values, residual, cotangent, filters, gain, spans)


def solution(mesh):
    split = P("seq", "chan")
    return jax.shard_map(
        shards,
        mesh=mesh,
        in_specs=(split, split, split, split, split, split, P("chan"), P()),
        out_specs=(split,) * 6,
        check_vma=False,
    )
```

```python
import jax
import jax.numpy as jnp
import ml_dtypes
import numpy as np
from jax import lax
from jax.experimental import pallas as pl
from jax.experimental.pallas import tpu as pltpu
from jax.sharding import PartitionSpec as P

D = 4096
BLOCK = 512
TOKENS = 16384
DOCS = 4
EPSILON = 1e-06
BLOCKS = TOKENS // BLOCK
FREQS = BLOCK
SPEC = 2 * FREQS
TILE = 4
GROUP = 4
PAD = TILE
ROWS = BLOCKS + PAD * (DOCS + 2)
LAG_PAD = TILE
LAG_ROWS = LAG_PAD + BLOCKS
F32 = jnp.float32
BF16 = jnp.bfloat16


def window_table():
    places = np.arange(BLOCK, dtype=np.int64)
    odd = 2 * np.arange(FREQS, dtype=np.int64) + 1
    phase = (places[:, None] * odd[None, :] % (4 * BLOCK)) * (np.pi / (2 * BLOCK))
    forward = np.concatenate([np.cos(phase), -np.sin(phase)], axis=1) / 8
    high = forward.astype(ml_dtypes.bfloat16)
    low = (forward - high.astype(np.float64)).astype(ml_dtypes.bfloat16)
    return np.concatenate([high, low])


def half_signs():
    lanes = lax.broadcasted_iota(jnp.int32, (1, 1, FREQS), 2)
    return (1 - 2 * (lanes % 2)).astype(F32)


def block_rows(slabs):
    count, chans, width = slabs.shape
    pairs = slabs.reshape(count // 2, 2, chans, width)
    joined = jnp.concatenate([pairs[:, 0], pairs[:, 1]], axis=2)
    return joined.reshape(count // 2 * chans, 2 * width)


def sender_slabs(rows, chans):
    width = rows.shape[1] // 2
    blocks = rows.reshape(rows.shape[0] // chans, 1, chans, 2 * width)
    joined = jnp.concatenate([blocks[..., :width], blocks[..., width:]], axis=1)
    return joined.reshape(2 * blocks.shape[0], chans, width)


def to_spectrum(rows, table_ref):
    rows = rows.astype(BF16)
    return jnp.dot(jnp.concatenate([rows, rows], axis=1), table_ref[...], preferred_element_type=F32)


def from_spectrum(spec, table_ref):
    across = (((1,), (1,)), ((), ()))
    return lax.dot_general(spec.astype(BF16), table_ref[pl.ds(0, BLOCK)], across, preferred_element_type=F32)


def doc_bounds(spans_ref, doc):
    return spans_ref[2 * doc] // BLOCK, spans_ref[2 * doc + 1] // BLOCK


COLUMNS = range(0, FREQS, 128)


def load_tile(ref, row):
    return tuple(
        tuple(
            (ref[row + i, :, pl.ds(lane, 128)], ref[row + i, :, pl.ds(FREQS + lane, 128)])
            for i in range(TILE)
        )
        for lane in COLUMNS
    )


def store_tile(ref, row, sums):
    for lane, column in zip(COLUMNS, sums):
        for i, (real, imag) in enumerate(column):
            ref[row + i, :, pl.ds(lane, 128)] = real
            ref[row + i, :, pl.ds(FREQS + lane, 128)] = imag


def zero_sums():
    zero = jnp.zeros((8, 128), F32)
    return tuple(tuple((zero, zero) for _ in range(TILE)) for _ in COLUMNS)


def add_rows(sums, rows_ref, rows, taps_ref, tap, conj, triangle=False):
    out = []
    for lane, column in zip(COLUMNS, sums):
        re_lanes, im_lanes = pl.ds(lane, 128), pl.ds(FREQS + lane, 128)
        column, seen = list(column), {}
        for j, row in enumerate(rows):
            a, b = rows_ref[row, :, re_lanes], rows_ref[row, :, im_lanes]
            for i in range(TILE):
                offset = j - i if conj else i - j
                if triangle and offset < 0:
                    continue
                if offset not in seen:
                    seen[offset] = (taps_ref[tap + offset, :, re_lanes], taps_ref[tap + offset, :, im_lanes])
                c, d = seen[offset]
                real, imag = column[i]
                if conj:
                    column[i] = (real + (c * a + d * b), imag + (c * b - d * a))
                else:
                    column[i] = (real + (c * a - d * b), imag + (c * b + d * a))
        out.append(tuple(column))
    return tuple(out)


def add_range(sums, count, step):
    count = jnp.maximum(count, 0)
    full = count // GROUP
    sums = lax.fori_loop(0, full, lambda g, sums: step(sums, GROUP * g, GROUP), sums)
    return lax.fori_loop(GROUP * full, count, lambda k, sums: step(sums, k, 1), sums)


def zero_gaps(spans_ref, ref, shift):
    for doc in range(DOCS - 1):
        _, end = doc_bounds(spans_ref, doc)
        start, _ = doc_bounds(spans_ref, doc + 1)

        @pl.loop(end, start)
        def _(n):
            ref[n + shift] = jnp.zeros(ref.shape[1:], F32)


def tiles(length):
    return (length + TILE - 1) // TILE


CHUNKS = 2


def gate_kernel(values_hbm, gate_hbm, filters_hbm, out_hbm, values_ref, gate_ref, filters_ref, out_ref, sems, out_sems):
    width = values_ref.shape[1] // CHUNKS
    slabs, twice, tokens = out_ref.shape
    slabs //= CHUNKS
    shape = (slabs, twice // 2, tokens)
    arriving = []
    for chunk in range(CHUNKS):
        lanes = pl.ds(chunk * width, width)
        arriving.append(
            [
                pltpu.make_async_copy(hbm.at[:, lanes], ref.at[:, lanes], sems.at[k, chunk])
                for k, (hbm, ref) in enumerate(
                    ((values_hbm, values_ref), (gate_hbm, gate_ref), (filters_hbm, filters_ref))
                )
            ]
        )
        for copy in arriving[-1]:
            copy.start()
    leaving = []
    for chunk in range(CHUNKS):
        lanes, rows = pl.ds(chunk * width, width), pl.ds(chunk * slabs, slabs)
        for copy in arriving[chunk]:
            copy.wait()
        gated = values_ref[:, lanes].astype(F32) * gate_ref[:, lanes].astype(F32)
        both = jnp.concatenate(
            [gated.T.reshape(shape), filters_ref[:, lanes].T.reshape(shape)], axis=1
        )
        out_ref[rows] = both.astype(BF16)
        leaving.append(pltpu.make_async_copy(out_ref.at[rows], out_hbm.at[rows], out_sems.at[chunk]))
        leaving[-1].start()
    for copy in leaving:
        copy.wait()


def stage_kernel(residual_hbm, gate_hbm, cotangent_hbm, staged_ref, sems):
    copies = [
        pltpu.make_async_copy(hbm, staged_ref.at[k], sems.at[k])
        for k, hbm in enumerate((residual_hbm, gate_hbm, cotangent_hbm))
    ]
    for copy in copies:
        copy.start()
    for copy in copies:
        copy.wait()


def forward_kernel(spans_ref, slabs_ref, table_ref, conv_ref, source_ref, taps_ref, spec_ref):
    signs = half_signs()
    both = to_spectrum(block_rows(slabs_ref[...]), table_ref).reshape(BLOCKS, 16, SPEC)
    spec_ref[pl.ds(0, BLOCKS)] = both[:, :8]
    real, imag = both[:, 8:, :FREQS], both[:, 8:, FREQS:]
    nothing = jnp.zeros((1, 8, FREQS), F32)
    before_real = jnp.concatenate([nothing, real[:-1]], axis=0)
    before_imag = jnp.concatenate([nothing, imag[:-1]], axis=0)
    taps_ref[pl.ds(0, LAG_PAD)] = jnp.zeros((LAG_PAD, 8, SPEC), F32)
    taps_ref[pl.ds(LAG_PAD, BLOCKS), :, :FREQS] = real - signs * before_imag
    taps_ref[pl.ds(LAG_PAD, BLOCKS), :, FREQS:] = imag + signs * before_real
    source_ref[...] = jnp.zeros((ROWS, 8, SPEC), F32)
    for doc in range(DOCS):
        start, end = doc_bounds(spans_ref, doc)

        @pl.loop(start, end)
        def _(n):
            source_ref[n + PAD * (doc + 1)] = spec_ref[n]

    zero_gaps(spans_ref, spec_ref, PAD)
    for doc in reversed(range(DOCS)):
        start, end = doc_bounds(spans_ref, doc)
        shift = PAD * (doc + 1)

        @pl.loop(0, tiles(end - start))
        def _(tile):
            first = end - TILE * (tile + 1)

            def step(sums, k, count):
                s = first - k - count
                rows = [s + shift + j for j in range(count)]
                return add_rows(sums, source_ref, rows, taps_ref, first - s + LAG_PAD, False)

            rows = [first + shift + j for j in range(TILE)]
            sums = add_rows(zero_sums(), source_ref, rows, taps_ref, LAG_PAD, False, triangle=True)
            store_tile(spec_ref, first + PAD, add_range(sums, first - start, step))

    total = spec_ref[pl.ds(PAD, BLOCKS)].reshape(BLOCKS * 8, SPEC)
    conv = from_spectrum(total, table_ref)
    conv_ref[...] = sender_slabs(conv, 8).astype(BF16)


def mixed_kernel(conv_ref, staged_ref, gain_ref, source_ref, taps_ref, mixed_ref, sums_ref):
    _, tokens, width = staged_ref.shape
    conv = conv_ref[...].astype(F32).reshape(width, tokens).T
    mixed = staged_ref[0].astype(F32) + conv * staged_ref[1].astype(F32)
    lifted = staged_ref[2].astype(F32) * gain_ref[...].astype(F32)
    mixed_ref[0] = mixed
    mixed_ref[1] = conv
    power = jnp.sum(mixed * mixed, axis=1, keepdims=True)
    inner = jnp.sum(lifted * mixed, axis=1, keepdims=True)
    lanes = lax.broadcasted_iota(jnp.int32, (tokens, 128), 1)
    both = jnp.where(lanes == 0, power, jnp.where(lanes == 1, inner, 0.0)).T[:2]
    sums_ref[...] = jnp.broadcast_to(both[None], sums_ref.shape)


def token_scales(sums_ref):
    total = jnp.sum(sums_ref[...], axis=0)
    padded = jnp.concatenate([total, jnp.zeros((126, total.shape[1]), F32)], axis=0).T
    scale = lax.rsqrt(padded[:, 0:1] / D + EPSILON)
    return scale, padded[:, 1:2] / D


def grad_kernel(sums_ref, mixed_ref, staged_ref, gain_ref, source_ref, taps_ref, grad_ref):
    scale, inner = token_scales(sums_ref)
    lifted = staged_ref[2].astype(F32) * gain_ref[...].astype(F32)
    mixed_grad = scale * (lifted - mixed_ref[0] * (scale * scale * inner))
    conv_grad = mixed_grad * staged_ref[1].astype(F32)
    grad_ref[...] = conv_grad.T.reshape(grad_ref.shape).astype(BF16)


def token_kernel(sums_ref, mixed_ref, staged_ref, gain_ref, normed_ref, residual_grad_ref, gate_grad_ref):
    scale, inner = token_scales(sums_ref)
    gain = gain_ref[...].astype(F32)
    mixed = mixed_ref[0]
    lifted = staged_ref[2].astype(F32) * gain
    normed_ref[...] = (mixed * scale * gain).astype(BF16)
    mixed_grad = scale * (lifted - mixed * (scale * scale * inner))
    residual_grad_ref[...] = mixed_grad.astype(BF16)
    gate_grad_ref[...] = (mixed_grad * mixed_ref[1]).astype(BF16)


def backward_kernel(spans_ref, slabs_ref, source_ref, taps_ref, table_ref, mixed_ref, out_ref, up_ref, spec_ref, lag_ref):
    signs = half_signs()
    up = to_spectrum(block_rows(slabs_ref[...].astype(F32)), table_ref)
    spec_ref[pl.ds(0, BLOCKS)] = up.reshape(BLOCKS, 8, SPEC)
    up_ref[...] = jnp.zeros((ROWS, 8, SPEC), F32)
    for doc in range(DOCS):
        start, end = doc_bounds(spans_ref, doc)

        @pl.loop(start, end)
        def _(n):
            up_ref[n + PAD * (doc + 1)] = spec_ref[n]

    zero_gaps(spans_ref, spec_ref, 0)
    for doc in range(DOCS):
        start, end = doc_bounds(spans_ref, doc)
        shift = PAD * (doc + 1)

        @pl.loop(0, tiles(end - start))
        def _(tile):
            first = start + TILE * tile

            def step(sums, k, count):
                rows = [first + TILE + k + shift + j for j in range(count)]
                return add_rows(sums, up_ref, rows, taps_ref, TILE + k + LAG_PAD, True)

            rows = [first + shift + j for j in range(TILE)]
            sums = add_rows(zero_sums(), up_ref, rows, taps_ref, LAG_PAD, True, triangle=True)
            store_tile(spec_ref, first, add_range(sums, end - first - TILE, step))

    lag_ref[...] = jnp.zeros(lag_ref.shape, F32)
    for doc in range(DOCS):
        start, end = doc_bounds(spans_ref, doc)
        begin = start + PAD * (doc + 1)

        @pl.loop(0, tiles(end - start))
        def _(tile):
            first = TILE * tile

            def step(sums, k, count):
                rows = [begin + first + TILE + k + j for j in range(count)]
                return add_rows(sums, up_ref, rows, source_ref, begin + TILE + k, True)

            rows = [begin + first + j for j in range(TILE)]
            sums = add_rows(load_tile(lag_ref, first), up_ref, rows, source_ref, begin, True, triangle=True)
            store_tile(lag_ref, first, add_range(sums, end - start - first - TILE, step))

    source_grad = from_spectrum(spec_ref[pl.ds(0, BLOCKS)].reshape(BLOCKS * 8, SPEC), table_ref)
    lags, later = lag_ref[pl.ds(0, BLOCKS)], lag_ref[pl.ds(1, BLOCKS)]
    folded = jnp.concatenate(
        [
            lags[..., :FREQS] + signs * later[..., FREQS:],
            lags[..., FREQS:] - signs * later[..., :FREQS],
        ],
        axis=2,
    )
    tap_grad = from_spectrum(folded.reshape(BLOCKS * 8, SPEC), table_ref)
    out_ref[...] = jnp.concatenate(
        [
            sender_slabs(source_grad, 8),
            sender_slabs(tap_grad * TOKENS**-0.5, 8),
        ],
        axis=1,
    ).astype(BF16)


def product_kernel(slabs_ref, values_ref, gate_ref, gate_grad_hbm, values_grad_hbm, filter_grad_hbm, gate_grad_ref, values_grad_ref, filter_grad_ref, sems):
    tokens, width = values_ref.shape
    part = tokens // 2
    leaving = []
    for k in range(2):
        rows = pl.ds(k * part, part)
        slabs = slabs_ref[:, :, rows].astype(F32)
        gated_grad = slabs[:, :8].reshape(width, part).T
        filter_grad_ref[rows] = slabs[:, 8:].reshape(width, part).T
        gate_grad_ref[rows] = (gated_grad * values_ref[rows].astype(F32)).astype(BF16)
        values_grad_ref[rows] = (gated_grad * gate_ref[rows].astype(F32)).astype(BF16)
        for which, (ref, hbm) in enumerate(
            (
                (filter_grad_ref, filter_grad_hbm),
                (gate_grad_ref, gate_grad_hbm),
                (values_grad_ref, values_grad_hbm),
            )
        ):
            leaving.append(pltpu.make_async_copy(ref.at[rows], hbm.at[rows], sems.at[which, k]))
            leaving[-1].start()
    for copy in leaving:
        copy.wait()


def call(kernel, ins, outs, scratch=(), limit=24, cost=4_000_000):
    spaces = {"v": pltpu.VMEM, "h": pltpu.HBM, "s": pltpu.SMEM}
    spec = lambda space: pl.BlockSpec(memory_space=spaces[space])
    return pl.pallas_call(
        kernel,
        out_shape=[
            pltpu.HBM(*shape) if space == "h" else jax.ShapeDtypeStruct(*shape)
            for shape, space in outs
        ],
        in_specs=[spec(space) for space in ins],
        out_specs=[spec(space) for _, space in outs],
        scratch_shapes=list(scratch),
        compiler_params=pltpu.CompilerParams(vmem_limit_bytes=limit * 1024 * 1024),
        cost_estimate=pl.CostEstimate(flops=cost, bytes_accessed=cost, transcendentals=0),
    )


def in_hbm(*arrays):
    return [pltpu.with_memory_space_constraint(array, pltpu.HBM) for array in arrays]


def exchange(array, axis):
    return lax.all_to_all(array, axis, split_axis=0, concat_axis=0, tiled=True)


SOURCE = ((ROWS, 8, SPEC), F32)
LAGS = ((LAG_ROWS, 8, SPEC), F32)
SUMS = ((PAD + BLOCKS, 8, SPEC), F32)


def vmem(shape):
    return pltpu.VMEM(*shape)


def run_forward(spans, slabs, table):
    single = ((slabs.shape[0], 8, slabs.shape[2]), BF16)
    return call(
        forward_kernel,
        "svv",
        [(single, "v"), (SOURCE, "v"), (LAGS, "v")],
        [vmem(SUMS)],
    )(spans, slabs, table)


def run_backward(spans, slabs, source, taps, table, mixed):
    pair = ((slabs.shape[0], 16, slabs.shape[2]), BF16)
    return call(
        backward_kernel,
        "svvvvv",
        [(pair, "v")],
        [vmem(SOURCE), vmem(SUMS), vmem(SUMS)],
    )(spans, slabs, source, taps, table, mixed)[0]


def body(exchange, input_gate, output_gate, values, residual, cotangent, filters, gain, spans):
    tokens, width = input_gate.shape
    table = jnp.asarray(window_table())
    like, wide = ((tokens, width), BF16), ((tokens, width), F32)
    pair, single = ((64, 16, tokens), BF16), ((64, 8, tokens), BF16)
    sums_rows = ((8, 2, tokens), F32)
    dma = pltpu.SemaphoreType.DMA

    (outgoing,) = call(
        gate_kernel,
        "hhh",
        [(pair, "h")],
        [vmem(like), vmem(like), vmem(wide), vmem(pair), dma((3, CHUNKS)), dma((CHUNKS,))],
    )(*in_hbm(values, input_gate, filters))
    incoming = exchange(outgoing, "seq")
    (staged,) = call(stage_kernel, "hhh", [(((3, tokens, width), BF16), "v")], [dma((3,))])(
        *in_hbm(residual, output_gate, cotangent)
    )
    incoming, staged, gain = lax.optimization_barrier((incoming, staged, gain))
    conv, source, taps = run_forward(spans, incoming, table)
    conv = exchange(conv, "seq")
    mixed, sums = call(
        mixed_kernel, "vvvvv", [(((2, tokens, width), F32), "v"), (sums_rows, "v")]
    )(conv, staged, gain, source, taps)
    sums = exchange(sums, "chan")
    (conv_grad,) = call(grad_kernel, "vvvvvv", [(single, "v")])(sums, mixed, staged, gain, source, taps)
    conv_grad = exchange(conv_grad, "seq")
    normed, residual_grad, output_gate_grad = call(token_kernel, "vvvv", [(like, "v")] * 3)(
        sums, mixed, staged, gain
    )
    grads = run_backward(spans, conv_grad, source, taps, table, mixed)
    grads = exchange(grads, "seq")
    input_gate_grad, values_grad, filter_grad = call(
        product_kernel,
        "vvv",
        [(like, "h"), (like, "h"), (wide, "h")],
        [vmem(like), vmem(like), vmem(wide), dma((3, 2))],
    )(grads, values, input_gate)
    return (normed, residual_grad, input_gate_grad, output_gate_grad, values_grad, filter_grad)


def shards(input_gate, output_gate, values, residual, cotangent, filters, norm_gain, doc_spans):
    gain = norm_gain.reshape(1, norm_gain.shape[0])
    spans = doc_spans.reshape(2 * DOCS)
    return body(exchange, input_gate, output_gate, values, residual, cotangent, filters, gain, spans)


def solution(mesh):
    split = P("seq", "chan")
    return jax.shard_map(
        shards,
        mesh=mesh,
        in_specs=(split, split, split, split, split, split, P("chan"), P()),
        out_specs=(split,) * 6,
        check_vma=False,
    )
```

```python
import jax
import jax.numpy as jnp
import ml_dtypes
import numpy as np
from jax import lax
from jax.experimental import pallas as pl
from jax.experimental.pallas import tpu as pltpu
from jax.sharding import PartitionSpec as P

D = 4096
BLOCK = 512
TOKENS = 16384
DOCS = 4
EPSILON = 1e-06
BLOCKS = TOKENS // BLOCK
FREQS = BLOCK
SPEC = 2 * FREQS
TILE = 4
PAD = TILE
ROWS = BLOCKS + PAD * (DOCS + 2)
LAG_PAD = TILE
LAG_ROWS = LAG_PAD + BLOCKS
F32 = jnp.float32
BF16 = jnp.bfloat16


def window_table():
    places = np.arange(BLOCK, dtype=np.int64)
    odd = 2 * np.arange(FREQS, dtype=np.int64) + 1
    phase = (places[:, None] * odd[None, :] % (4 * BLOCK)) * (np.pi / (2 * BLOCK))
    forward = np.concatenate([np.cos(phase), -np.sin(phase)], axis=1) / 8
    high = forward.astype(ml_dtypes.bfloat16)
    low = (forward - high.astype(np.float64)).astype(ml_dtypes.bfloat16)
    return np.concatenate([high, low])


def half_signs():
    lanes = lax.broadcasted_iota(jnp.int32, (1, 1, FREQS), 2)
    return (1 - 2 * (lanes % 2)).astype(F32)


def block_rows(slabs):
    count, chans, width = slabs.shape
    pairs = slabs.reshape(count // 2, 2, chans, width)
    joined = jnp.concatenate([pairs[:, 0], pairs[:, 1]], axis=2)
    return joined.reshape(count // 2 * chans, 2 * width)


def sender_slabs(rows, chans):
    width = rows.shape[1] // 2
    blocks = rows.reshape(rows.shape[0] // chans, 1, chans, 2 * width)
    joined = jnp.concatenate([blocks[..., :width], blocks[..., width:]], axis=1)
    return joined.reshape(2 * blocks.shape[0], chans, width)


def to_spectrum(rows, table_ref):
    rows = rows.astype(BF16)
    return jnp.dot(jnp.concatenate([rows, rows], axis=1), table_ref[...], preferred_element_type=F32)


def from_spectrum(spec, table_ref):
    across = (((1,), (1,)), ((), ()))
    return lax.dot_general(spec.astype(BF16), table_ref[pl.ds(0, BLOCK)], across, preferred_element_type=F32)


def doc_bounds(spans_ref, doc):
    return spans_ref[2 * doc] // BLOCK, spans_ref[2 * doc + 1] // BLOCK


COLUMNS = range(0, FREQS, 128)


def load_tile(ref, row):
    return tuple(
        tuple(
            (ref[row + i, :, pl.ds(lane, 128)], ref[row + i, :, pl.ds(FREQS + lane, 128)])
            for i in range(TILE)
        )
        for lane in COLUMNS
    )


def store_tile(ref, row, sums):
    for lane, column in zip(COLUMNS, sums):
        for i, (real, imag) in enumerate(column):
            ref[row + i, :, pl.ds(lane, 128)] = real
            ref[row + i, :, pl.ds(FREQS + lane, 128)] = imag


def zero_sums():
    zero = jnp.zeros((8, 128), F32)
    return tuple(tuple((zero, zero) for _ in range(TILE)) for _ in COLUMNS)


def add_rows(sums, rows_ref, rows, taps_ref, tap, conj, triangle=False):
    out = []
    for lane, column in zip(COLUMNS, sums):
        re_lanes, im_lanes = pl.ds(lane, 128), pl.ds(FREQS + lane, 128)
        column, seen = list(column), {}
        for j, row in enumerate(rows):
            a, b = rows_ref[row, :, re_lanes], rows_ref[row, :, im_lanes]
            for i in range(TILE):
                offset = j - i if conj else i - j
                if triangle and offset < 0:
                    continue
                if offset not in seen:
                    seen[offset] = (taps_ref[tap + offset, :, re_lanes], taps_ref[tap + offset, :, im_lanes])
                c, d = seen[offset]
                real, imag = column[i]
                if conj:
                    column[i] = (real + (c * a + d * b), imag + (c * b - d * a))
                else:
                    column[i] = (real + (c * a - d * b), imag + (c * b + d * a))
        out.append(tuple(column))
    return tuple(out)


def product(c, d, a, b, conj):
    if conj:
        return c * a + d * b, c * b - d * a
    return c * a - d * b, c * b + d * a


def add_group(sums, rows_ref, row, taps_ref, tap, conj):
    apart = taps_ref.shape[0] // 2
    out = []
    for lane, column in zip(COLUMNS, sums):
        re_lanes, im_lanes = pl.ds(lane, 128), pl.ds(FREQS + lane, 128)

        def at(ref, place):
            return ref[place, :, re_lanes], ref[place, :, im_lanes]

        ups = [at(rows_ref, row + j) for j in range(TILE)]
        both = [(ups[j][0] + ups[j + 2][0], ups[j][1] + ups[j + 2][1]) for j in range(2)]
        shared = {o: at(taps_ref, tap + o) for o in range(-1, 2)}
        apart_taps = {o: at(taps_ref, apart + tap + o) for o in range(-3, 2)}
        column = list(column)
        for i in range(2):
            real = imag = 0.0
            for j in range(2):
                o = j - i if conj else i - j
                re, im = product(*shared[o], *both[j], conj)
                real, imag = real + re, imag + im
            low, high = column[i], column[i + 2]
            low, high = (low[0] + real, low[1] + imag), (high[0] + real, high[1] + imag)
            for j in range(2):
                o = j - i if conj else i - j
                more, less = (ups[j + 2], ups[j]) if conj else (ups[j], ups[j + 2])
                re, im = product(*apart_taps[o], *more, conj)
                re_less, im_less = product(*apart_taps[o - 2], *less, conj)
                if conj:
                    low, high = (low[0] + re, low[1] + im), (high[0] - re_less, high[1] - im_less)
                else:
                    low, high = (low[0] - re_less, low[1] - im_less), (high[0] + re, high[1] + im)
            column[i], column[i + 2] = low, high
        out.append(tuple(column))
    return tuple(out)


def store_apart(ref):
    half = ref.shape[0] // 2
    ref[pl.ds(half, half - 2)] = ref[pl.ds(2, half - 2)] - ref[pl.ds(0, half - 2)]


def add_range(sums, count, step):
    count = jnp.maximum(count, 0)
    full = count // TILE
    sums = lax.fori_loop(0, full, lambda g, sums: step(sums, TILE * g, TILE), sums)
    return lax.fori_loop(TILE * full, count, lambda k, sums: step(sums, k, 1), sums)


def zero_gaps(spans_ref, ref, shift):
    for doc in range(DOCS - 1):
        _, end = doc_bounds(spans_ref, doc)
        start, _ = doc_bounds(spans_ref, doc + 1)

        @pl.loop(end, start)
        def _(n):
            ref[n + shift] = jnp.zeros(ref.shape[1:], F32)


def tiles(length):
    return (length + TILE - 1) // TILE


CHUNKS = 2


def gate_kernel(values_hbm, gate_hbm, filters_hbm, out_hbm, values_ref, gate_ref, filters_ref, out_ref, sems, out_sems):
    width = values_ref.shape[1] // CHUNKS
    slabs, twice, tokens = out_ref.shape
    slabs //= CHUNKS
    shape = (slabs, twice // 2, tokens)
    arriving = []
    for chunk in range(CHUNKS):
        lanes = pl.ds(chunk * width, width)
        arriving.append(
            [
                pltpu.make_async_copy(hbm.at[:, lanes], ref.at[:, lanes], sems.at[k, chunk])
                for k, (hbm, ref) in enumerate(
                    ((values_hbm, values_ref), (gate_hbm, gate_ref), (filters_hbm, filters_ref))
                )
            ]
        )
        for copy in arriving[-1]:
            copy.start()
    leaving = []
    for chunk in range(CHUNKS):
        lanes, rows = pl.ds(chunk * width, width), pl.ds(chunk * slabs, slabs)
        for copy in arriving[chunk]:
            copy.wait()
        gated = values_ref[:, lanes].astype(F32) * gate_ref[:, lanes].astype(F32)
        both = jnp.concatenate(
            [gated.T.reshape(shape), filters_ref[:, lanes].T.reshape(shape)], axis=1
        )
        out_ref[rows] = both.astype(BF16)
        leaving.append(pltpu.make_async_copy(out_ref.at[rows], out_hbm.at[rows], out_sems.at[chunk]))
        leaving[-1].start()
    for copy in leaving:
        copy.wait()


def stage_kernel(residual_hbm, gate_hbm, cotangent_hbm, table_hbm, staged_ref, table_ref, sems):
    copies = [
        pltpu.make_async_copy(hbm, staged_ref.at[k], sems.at[k])
        for k, hbm in enumerate((residual_hbm, gate_hbm, cotangent_hbm))
    ]
    copies.append(pltpu.make_async_copy(table_hbm, table_ref, sems.at[3]))
    for copy in copies:
        copy.start()
    for copy in copies:
        copy.wait()


def forward_kernel(spans_ref, slabs_ref, table_ref, conv_ref, source_ref, taps_ref, spec_ref):
    signs = half_signs()
    both = to_spectrum(block_rows(slabs_ref[...]), table_ref).reshape(BLOCKS, 16, SPEC)
    spec_ref[pl.ds(0, BLOCKS)] = both[:, :8]
    real, imag = both[:, 8:, :FREQS], both[:, 8:, FREQS:]
    nothing = jnp.zeros((1, 8, FREQS), F32)
    before_real = jnp.concatenate([nothing, real[:-1]], axis=0)
    before_imag = jnp.concatenate([nothing, imag[:-1]], axis=0)
    taps_ref[pl.ds(0, LAG_PAD)] = jnp.zeros((LAG_PAD, 8, SPEC), F32)
    taps_ref[pl.ds(LAG_PAD, BLOCKS), :, :FREQS] = real - signs * before_imag
    taps_ref[pl.ds(LAG_PAD, BLOCKS), :, FREQS:] = imag + signs * before_real
    store_apart(taps_ref)
    source_ref[pl.ds(0, ROWS)] = jnp.zeros((ROWS, 8, SPEC), F32)
    for doc in range(DOCS):
        start, end = doc_bounds(spans_ref, doc)

        @pl.loop(start, end)
        def _(n):
            source_ref[n + PAD * (doc + 1)] = spec_ref[n]

    store_apart(source_ref)
    zero_gaps(spans_ref, spec_ref, PAD)
    for doc in reversed(range(DOCS)):
        start, end = doc_bounds(spans_ref, doc)
        shift = PAD * (doc + 1)

        @pl.loop(0, tiles(end - start))
        def _(tile):
            first = end - TILE * (tile + 1)

            def step(sums, k, count):
                s = first - k - count
                if count == TILE:
                    return add_group(sums, source_ref, s + shift, taps_ref, first - s + LAG_PAD, False)
                rows = [s + shift + j for j in range(count)]
                return add_rows(sums, source_ref, rows, taps_ref, first - s + LAG_PAD, False)

            rows = [first + shift + j for j in range(TILE)]
            sums = add_rows(zero_sums(), source_ref, rows, taps_ref, LAG_PAD, False, triangle=True)
            store_tile(spec_ref, first + PAD, add_range(sums, first - start, step))

    total = spec_ref[pl.ds(PAD, BLOCKS)].reshape(BLOCKS * 8, SPEC)
    conv = from_spectrum(total, table_ref)
    conv_ref[...] = sender_slabs(conv, 8).astype(BF16)


def mixed_kernel(conv_ref, staged_ref, gain_ref, source_ref, taps_ref, table_ref, mixed_ref, sums_ref):
    _, tokens, width = staged_ref.shape
    conv = conv_ref[...].astype(F32).reshape(width, tokens).T
    mixed = staged_ref[0].astype(F32) + conv * staged_ref[1].astype(F32)
    lifted = staged_ref[2].astype(F32) * gain_ref[...].astype(F32)
    mixed_ref[0] = mixed
    mixed_ref[1] = conv
    power = jnp.sum(mixed * mixed, axis=1, keepdims=True)
    inner = jnp.sum(lifted * mixed, axis=1, keepdims=True)
    lanes = lax.broadcasted_iota(jnp.int32, (tokens, 128), 1)
    both = jnp.where(lanes == 0, power, jnp.where(lanes == 1, inner, 0.0)).T[:2]
    sums_ref[...] = jnp.broadcast_to(both[None], sums_ref.shape)


def token_scales(sums_ref):
    total = jnp.sum(sums_ref[...], axis=0)
    padded = jnp.concatenate([total, jnp.zeros((126, total.shape[1]), F32)], axis=0).T
    scale = lax.rsqrt(padded[:, 0:1] / D + EPSILON)
    return scale, padded[:, 1:2] / D


def grad_kernel(sums_ref, mixed_ref, staged_ref, gain_ref, source_ref, taps_ref, table_ref, grad_ref):
    scale, inner = token_scales(sums_ref)
    lifted = staged_ref[2].astype(F32) * gain_ref[...].astype(F32)
    mixed_grad = scale * (lifted - mixed_ref[0] * (scale * scale * inner))
    conv_grad = mixed_grad * staged_ref[1].astype(F32)
    grad_ref[...] = conv_grad.T.reshape(grad_ref.shape).astype(BF16)


def token_kernel(sums_ref, mixed_ref, staged_ref, gain_ref, normed_ref, residual_grad_ref, gate_grad_ref):
    scale, inner = token_scales(sums_ref)
    gain = gain_ref[...].astype(F32)
    mixed = mixed_ref[0]
    lifted = staged_ref[2].astype(F32) * gain
    normed_ref[...] = (mixed * scale * gain).astype(BF16)
    mixed_grad = scale * (lifted - mixed * (scale * scale * inner))
    residual_grad_ref[...] = mixed_grad.astype(BF16)
    gate_grad_ref[...] = (mixed_grad * mixed_ref[1]).astype(BF16)


def backward_kernel(spans_ref, slabs_ref, source_ref, taps_ref, table_ref, mixed_ref, out_hbm, out_ref, up_ref, spec_ref, lag_ref, sem):
    signs = half_signs()
    up = to_spectrum(block_rows(slabs_ref[...].astype(F32)), table_ref)
    spec_ref[pl.ds(0, BLOCKS)] = up.reshape(BLOCKS, 8, SPEC)
    up_ref[...] = jnp.zeros((ROWS, 8, SPEC), F32)
    for doc in range(DOCS):
        start, end = doc_bounds(spans_ref, doc)

        @pl.loop(start, end)
        def _(n):
            up_ref[n + PAD * (doc + 1)] = spec_ref[n]

    zero_gaps(spans_ref, spec_ref, 0)
    for doc in range(DOCS):
        start, end = doc_bounds(spans_ref, doc)
        shift = PAD * (doc + 1)

        @pl.loop(0, tiles(end - start))
        def _(tile):
            first = start + TILE * tile

            def step(sums, k, count):
                if count == TILE:
                    return add_group(sums, up_ref, first + TILE + k + shift, taps_ref, TILE + k + LAG_PAD, True)
                rows = [first + TILE + k + shift + j for j in range(count)]
                return add_rows(sums, up_ref, rows, taps_ref, TILE + k + LAG_PAD, True)

            rows = [first + shift + j for j in range(TILE)]
            sums = add_rows(zero_sums(), up_ref, rows, taps_ref, LAG_PAD, True, triangle=True)
            store_tile(spec_ref, first, add_range(sums, end - first - TILE, step))

    lag_ref[...] = jnp.zeros(lag_ref.shape, F32)
    for doc in range(DOCS):
        start, end = doc_bounds(spans_ref, doc)
        begin = start + PAD * (doc + 1)

        @pl.loop(0, tiles(end - start))
        def _(tile):
            first = TILE * tile

            def step(sums, k, count):
                if count == TILE:
                    return add_group(sums, up_ref, begin + first + TILE + k, source_ref, begin + TILE + k, True)
                rows = [begin + first + TILE + k + j for j in range(count)]
                return add_rows(sums, up_ref, rows, source_ref, begin + TILE + k, True)

            rows = [begin + first + j for j in range(TILE)]
            sums = add_rows(load_tile(lag_ref, first), up_ref, rows, source_ref, begin, True, triangle=True)
            store_tile(lag_ref, first, add_range(sums, end - start - first - TILE, step))

    source_grad = from_spectrum(spec_ref[pl.ds(0, BLOCKS)].reshape(BLOCKS * 8, SPEC), table_ref)
    lags, later = lag_ref[pl.ds(0, BLOCKS)], lag_ref[pl.ds(1, BLOCKS)]
    folded = jnp.concatenate(
        [
            lags[..., :FREQS] + signs * later[..., FREQS:],
            lags[..., FREQS:] - signs * later[..., :FREQS],
        ],
        axis=2,
    )
    tap_grad = from_spectrum(folded.reshape(BLOCKS * 8, SPEC), table_ref)
    out_ref[...] = jnp.concatenate(
        [
            sender_slabs(source_grad, 8),
            sender_slabs(tap_grad * TOKENS**-0.5, 8),
        ],
        axis=1,
    ).astype(BF16)
    leaving = pltpu.make_async_copy(out_ref, out_hbm, sem)
    leaving.start()
    leaving.wait()


def product_kernel(slabs_ref, values_ref, gate_ref, gate_grad_hbm, values_grad_hbm, filter_grad_hbm, gate_grad_ref, values_grad_ref, filter_grad_ref, sems):
    tokens, width = values_ref.shape
    part = tokens // 2
    leaving = []
    for k in range(2):
        rows = pl.ds(k * part, part)
        slabs = slabs_ref[:, :, rows].astype(F32)
        gated_grad = slabs[:, :8].reshape(width, part).T
        filter_grad_ref[rows] = slabs[:, 8:].reshape(width, part).T
        gate_grad_ref[rows] = (gated_grad * values_ref[rows].astype(F32)).astype(BF16)
        values_grad_ref[rows] = (gated_grad * gate_ref[rows].astype(F32)).astype(BF16)
        for which, (ref, hbm) in enumerate(
            (
                (filter_grad_ref, filter_grad_hbm),
                (gate_grad_ref, gate_grad_hbm),
                (values_grad_ref, values_grad_hbm),
            )
        ):
            leaving.append(pltpu.make_async_copy(ref.at[rows], hbm.at[rows], sems.at[which, k]))
            leaving[-1].start()
    for copy in leaving:
        copy.wait()


def call(kernel, ins, outs, scratch=(), limit=24, cost=4_000_000):
    spaces = {"v": pltpu.VMEM, "h": pltpu.HBM, "s": pltpu.SMEM}
    spec = lambda space: pl.BlockSpec(memory_space=spaces[space])
    return pl.pallas_call(
        kernel,
        out_shape=[
            pltpu.HBM(*shape) if space == "h" else jax.ShapeDtypeStruct(*shape)
            for shape, space in outs
        ],
        in_specs=[spec(space) for space in ins],
        out_specs=[spec(space) for _, space in outs],
        scratch_shapes=list(scratch),
        compiler_params=pltpu.CompilerParams(vmem_limit_bytes=limit * 1024 * 1024),
        cost_estimate=pl.CostEstimate(flops=cost, bytes_accessed=cost, transcendentals=0),
    )


def in_hbm(*arrays):
    return [pltpu.with_memory_space_constraint(array, pltpu.HBM) for array in arrays]


def exchange(array, axis):
    return lax.all_to_all(array, axis, split_axis=0, concat_axis=0, tiled=True)


UPS = ((ROWS, 8, SPEC), F32)
SOURCE = ((2 * ROWS, 8, SPEC), F32)
LAGS = ((2 * LAG_ROWS, 8, SPEC), F32)
SUMS = ((PAD + BLOCKS, 8, SPEC), F32)


def vmem(shape):
    return pltpu.VMEM(*shape)


def run_forward(spans, slabs, table):
    single = ((slabs.shape[0], 8, slabs.shape[2]), BF16)
    return call(
        forward_kernel,
        "svv",
        [(single, "v"), (SOURCE, "v"), (LAGS, "v")],
        [vmem(SUMS)],
    )(spans, slabs, table)


def run_backward(spans, slabs, source, taps, table, mixed):
    pair = ((slabs.shape[0], 16, slabs.shape[2]), BF16)
    return call(
        backward_kernel,
        "svvvvv",
        [(pair, "h")],
        [vmem(pair), vmem(UPS), vmem(SUMS), vmem(SUMS), pltpu.SemaphoreType.DMA],
    )(spans, slabs, source, taps, table, mixed)[0]


def body(exchange, input_gate, output_gate, values, residual, cotangent, filters, gain, spans):
    tokens, width = input_gate.shape
    table = jnp.asarray(window_table())
    like, wide = ((tokens, width), BF16), ((tokens, width), F32)
    pair, single = ((64, 16, tokens), BF16), ((64, 8, tokens), BF16)
    sums_rows = ((8, 2, tokens), F32)
    dma = pltpu.SemaphoreType.DMA

    (outgoing,) = call(
        gate_kernel,
        "hhh",
        [(pair, "h")],
        [vmem(like), vmem(like), vmem(wide), vmem(pair), dma((3, CHUNKS)), dma((CHUNKS,))],
    )(*in_hbm(values, input_gate, filters))
    incoming = exchange(outgoing, "seq")
    staged, table = call(
        stage_kernel,
        "hhhh",
        [(((3, tokens, width), BF16), "v"), ((table.shape, BF16), "v")],
        [dma((4,))],
    )(*in_hbm(residual, output_gate, cotangent, table))
    incoming, staged, table, gain = lax.optimization_barrier((incoming, staged, table, gain))
    conv, source, taps = run_forward(spans, incoming, table)
    conv = exchange(conv, "seq")
    mixed, sums = call(
        mixed_kernel, "vvvvvv", [(((2, tokens, width), F32), "v"), (sums_rows, "v")]
    )(conv, staged, gain, source, taps, table)
    sums = exchange(sums, "chan")
    (conv_grad,) = call(grad_kernel, "vvvvvvv", [(single, "v")])(sums, mixed, staged, gain, source, taps, table)
    conv_grad = exchange(conv_grad, "seq")
    normed, residual_grad, output_gate_grad = call(token_kernel, "vvvv", [(like, "v")] * 3)(
        sums, mixed, staged, gain
    )
    grads = run_backward(spans, conv_grad, source, taps, table, mixed)
    grads = exchange(grads, "seq")
    input_gate_grad, values_grad, filter_grad = call(
        product_kernel,
        "vvv",
        [(like, "h"), (like, "h"), (wide, "h")],
        [vmem(like), vmem(like), vmem(wide), dma((3, 2))],
    )(grads, values, input_gate)
    return (normed, residual_grad, input_gate_grad, output_gate_grad, values_grad, filter_grad)


def shards(input_gate, output_gate, values, residual, cotangent, filters, norm_gain, doc_spans):
    gain = norm_gain.reshape(1, norm_gain.shape[0])
    spans = doc_spans.reshape(2 * DOCS)
    return body(exchange, input_gate, output_gate, values, residual, cotangent, filters, gain, spans)


def solution(mesh):
    split = P("seq", "chan")
    return jax.shard_map(
        shards,
        mesh=mesh,
        in_specs=(split, split, split, split, split, split, P("chan"), P()),
        out_specs=(split,) * 6,
        check_vma=False,
    )
```

```python
import jax
import jax.numpy as jnp
import ml_dtypes
import numpy as np
from jax import lax
from jax.experimental import pallas as pl
from jax.experimental.pallas import tpu as pltpu
from jax.sharding import PartitionSpec as P

D = 4096
BLOCK = 512
TOKENS = 16384
DOCS = 4
EPSILON = 1e-06
BLOCKS = TOKENS // BLOCK
FREQS = BLOCK
SPEC = 2 * FREQS
TILE = 4
PAD = TILE
ROWS = BLOCKS + PAD * (DOCS + 2)
LAG_PAD = TILE
LAG_ROWS = LAG_PAD + BLOCKS
F32 = jnp.float32
BF16 = jnp.bfloat16


def window_table():
    places = np.arange(BLOCK, dtype=np.int64)
    odd = 2 * np.arange(FREQS, dtype=np.int64) + 1
    phase = (places[:, None] * odd[None, :] % (4 * BLOCK)) * (np.pi / (2 * BLOCK))
    forward = np.concatenate([np.cos(phase), -np.sin(phase)], axis=1) / 8
    high = forward.astype(ml_dtypes.bfloat16)
    low = (forward - high.astype(np.float64)).astype(ml_dtypes.bfloat16)
    return np.concatenate([high, low])


def half_signs():
    lanes = lax.broadcasted_iota(jnp.int32, (1, 1, FREQS), 2)
    return (1 - 2 * (lanes % 2)).astype(F32)


def block_rows(slabs):
    count, chans, width = slabs.shape
    pairs = slabs.reshape(count // 2, 2, chans, width)
    joined = jnp.concatenate([pairs[:, 0], pairs[:, 1]], axis=2)
    return joined.reshape(count // 2 * chans, 2 * width)


def sender_slabs(rows, chans):
    width = rows.shape[1] // 2
    blocks = rows.reshape(rows.shape[0] // chans, 1, chans, 2 * width)
    joined = jnp.concatenate([blocks[..., :width], blocks[..., width:]], axis=1)
    return joined.reshape(2 * blocks.shape[0], chans, width)


def to_spectrum(rows, table_ref):
    rows = rows.astype(BF16)
    return jnp.dot(jnp.concatenate([rows, rows], axis=1), table_ref[...], preferred_element_type=F32)


def from_spectrum(spec, table_ref):
    across = (((1,), (1,)), ((), ()))
    return lax.dot_general(spec.astype(BF16), table_ref[pl.ds(0, BLOCK)], across, preferred_element_type=F32)


def doc_bounds(spans_ref, doc):
    return spans_ref[2 * doc] // BLOCK, spans_ref[2 * doc + 1] // BLOCK


COLUMNS = range(0, FREQS, 128)


def load_tile(ref, row):
    return tuple(
        tuple(
            (ref[row + i, :, pl.ds(lane, 128)], ref[row + i, :, pl.ds(FREQS + lane, 128)])
            for i in range(TILE)
        )
        for lane in COLUMNS
    )


def store_tile(ref, row, sums):
    for lane, column in zip(COLUMNS, sums):
        for i, (real, imag) in enumerate(column):
            ref[row + i, :, pl.ds(lane, 128)] = real
            ref[row + i, :, pl.ds(FREQS + lane, 128)] = imag


def zero_sums():
    zero = jnp.zeros((8, 128), F32)
    return tuple(tuple((zero, zero) for _ in range(TILE)) for _ in COLUMNS)


def add_rows(sums, rows_ref, rows, taps_ref, tap, conj, triangle=False):
    out = []
    for lane, column in zip(COLUMNS, sums):
        re_lanes, im_lanes = pl.ds(lane, 128), pl.ds(FREQS + lane, 128)
        column, seen = list(column), {}
        for j, row in enumerate(rows):
            a, b = rows_ref[row, :, re_lanes], rows_ref[row, :, im_lanes]
            for i in range(TILE):
                offset = j - i if conj else i - j
                if triangle and offset < 0:
                    continue
                if offset not in seen:
                    seen[offset] = (taps_ref[tap + offset, :, re_lanes], taps_ref[tap + offset, :, im_lanes])
                c, d = seen[offset]
                real, imag = column[i]
                if conj:
                    column[i] = (real + (c * a + d * b), imag + (c * b - d * a))
                else:
                    column[i] = (real + (c * a - d * b), imag + (c * b + d * a))
        out.append(tuple(column))
    return tuple(out)


def product(c, d, a, b, conj):
    if conj:
        return c * a + d * b, c * b - d * a
    return c * a - d * b, c * b + d * a


def add_group(sums, rows_ref, row, taps_ref, tap, conj):
    apart = taps_ref.shape[0] // 2
    out = []
    for lane, column in zip(COLUMNS, sums):
        re_lanes, im_lanes = pl.ds(lane, 128), pl.ds(FREQS + lane, 128)

        def at(ref, place):
            return ref[place, :, re_lanes], ref[place, :, im_lanes]

        ups = [at(rows_ref, row + j) for j in range(TILE)]
        both = [(ups[j][0] + ups[j + 2][0], ups[j][1] + ups[j + 2][1]) for j in range(2)]
        shared = {o: at(taps_ref, tap + o) for o in range(-1, 2)}
        apart_taps = {o: at(taps_ref, apart + tap + o) for o in range(-3, 2)}
        column = list(column)
        for i in range(2):
            real = imag = 0.0
            for j in range(2):
                o = j - i if conj else i - j
                re, im = product(*shared[o], *both[j], conj)
                real, imag = real + re, imag + im
            low, high = column[i], column[i + 2]
            low, high = (low[0] + real, low[1] + imag), (high[0] + real, high[1] + imag)
            for j in range(2):
                o = j - i if conj else i - j
                more, less = (ups[j + 2], ups[j]) if conj else (ups[j], ups[j + 2])
                re, im = product(*apart_taps[o], *more, conj)
                re_less, im_less = product(*apart_taps[o - 2], *less, conj)
                if conj:
                    low, high = (low[0] + re, low[1] + im), (high[0] - re_less, high[1] - im_less)
                else:
                    low, high = (low[0] - re_less, low[1] - im_less), (high[0] + re, high[1] + im)
            column[i], column[i + 2] = low, high
        out.append(tuple(column))
    return tuple(out)


def store_apart(ref):
    half = ref.shape[0] // 2
    ref[pl.ds(half, half - 2)] = ref[pl.ds(2, half - 2)] - ref[pl.ds(0, half - 2)]


def add_range(sums, count, step):
    count = jnp.maximum(count, 0)
    full = count // TILE
    sums = lax.fori_loop(0, full, lambda g, sums: step(sums, TILE * g, TILE), sums)
    return lax.fori_loop(TILE * full, count, lambda k, sums: step(sums, k, 1), sums)


def zero_gaps(spans_ref, ref, shift):
    for doc in range(DOCS - 1):
        _, end = doc_bounds(spans_ref, doc)
        start, _ = doc_bounds(spans_ref, doc + 1)

        @pl.loop(end, start)
        def _(n):
            ref[n + shift] = jnp.zeros(ref.shape[1:], F32)


def tiles(length):
    return (length + TILE - 1) // TILE


CHUNKS = 2


def gate_kernel(values_hbm, gate_hbm, filters_hbm, out_hbm, values_ref, gate_ref, filters_ref, out_ref, sems, out_sems):
    width = values_ref.shape[1] // CHUNKS
    slabs, twice, tokens = out_ref.shape
    slabs //= CHUNKS
    shape = (slabs, twice // 2, tokens)
    arriving = []
    for chunk in range(CHUNKS):
        lanes = pl.ds(chunk * width, width)
        arriving.append(
            [
                pltpu.make_async_copy(hbm.at[:, lanes], ref.at[:, lanes], sems.at[k, chunk])
                for k, (hbm, ref) in enumerate(
                    ((values_hbm, values_ref), (gate_hbm, gate_ref), (filters_hbm, filters_ref))
                )
            ]
        )
        for copy in arriving[-1]:
            copy.start()
    leaving = []
    for chunk in range(CHUNKS):
        lanes, rows = pl.ds(chunk * width, width), pl.ds(chunk * slabs, slabs)
        for copy in arriving[chunk]:
            copy.wait()
        gated = values_ref[:, lanes].astype(F32) * gate_ref[:, lanes].astype(F32)
        both = jnp.concatenate(
            [gated.T.reshape(shape), filters_ref[:, lanes].T.reshape(shape)], axis=1
        )
        out_ref[rows] = both.astype(BF16)
        leaving.append(pltpu.make_async_copy(out_ref.at[rows], out_hbm.at[rows], out_sems.at[chunk]))
        leaving[-1].start()
    for copy in leaving:
        copy.wait()


def stage_kernel(residual_hbm, gate_hbm, cotangent_hbm, staged_ref, sems):
    copies = [
        pltpu.make_async_copy(hbm, staged_ref.at[k], sems.at[k])
        for k, hbm in enumerate((residual_hbm, gate_hbm, cotangent_hbm))
    ]
    for copy in copies:
        copy.start()
    for copy in copies:
        copy.wait()


def forward_kernel(spans_ref, slabs_ref, table_ref, conv_ref, source_ref, taps_ref, spec_ref):
    signs = half_signs()
    both = to_spectrum(block_rows(slabs_ref[...]), table_ref).reshape(BLOCKS, 16, SPEC)
    spec_ref[pl.ds(0, BLOCKS)] = both[:, :8]
    real, imag = both[:, 8:, :FREQS], both[:, 8:, FREQS:]
    nothing = jnp.zeros((1, 8, FREQS), F32)
    before_real = jnp.concatenate([nothing, real[:-1]], axis=0)
    before_imag = jnp.concatenate([nothing, imag[:-1]], axis=0)
    taps_ref[pl.ds(0, LAG_PAD)] = jnp.zeros((LAG_PAD, 8, SPEC), F32)
    taps_ref[pl.ds(LAG_PAD, BLOCKS), :, :FREQS] = real - signs * before_imag
    taps_ref[pl.ds(LAG_PAD, BLOCKS), :, FREQS:] = imag + signs * before_real
    store_apart(taps_ref)
    source_ref[pl.ds(0, ROWS)] = jnp.zeros((ROWS, 8, SPEC), F32)
    for doc in range(DOCS):
        start, end = doc_bounds(spans_ref, doc)

        @pl.loop(start, end)
        def _(n):
            source_ref[n + PAD * (doc + 1)] = spec_ref[n]

    store_apart(source_ref)
    zero_gaps(spans_ref, spec_ref, PAD)
    for doc in reversed(range(DOCS)):
        start, end = doc_bounds(spans_ref, doc)
        shift = PAD * (doc + 1)

        @pl.loop(0, tiles(end - start))
        def _(tile):
            first = end - TILE * (tile + 1)

            def step(sums, k, count):
                s = first - k - count
                if count == TILE:
                    return add_group(sums, source_ref, s + shift, taps_ref, first - s + LAG_PAD, False)
                rows = [s + shift + j for j in range(count)]
                return add_rows(sums, source_ref, rows, taps_ref, first - s + LAG_PAD, False)

            rows = [first + shift + j for j in range(TILE)]
            sums = add_rows(zero_sums(), source_ref, rows, taps_ref, LAG_PAD, False, triangle=True)
            store_tile(spec_ref, first + PAD, add_range(sums, first - start, step))

    total = spec_ref[pl.ds(PAD, BLOCKS)].reshape(BLOCKS * 8, SPEC)
    conv = from_spectrum(total, table_ref)
    conv_ref[...] = sender_slabs(conv, 8).astype(BF16)


def mixed_kernel(conv_ref, staged_ref, gain_ref, source_ref, taps_ref, mixed_ref, sums_ref):
    _, tokens, width = staged_ref.shape
    conv = conv_ref[...].astype(F32).reshape(width, tokens).T
    mixed = staged_ref[0].astype(F32) + conv * staged_ref[1].astype(F32)
    lifted = staged_ref[2].astype(F32) * gain_ref[...].astype(F32)
    mixed_ref[0] = mixed
    mixed_ref[1] = conv
    power = jnp.sum(mixed * mixed, axis=1, keepdims=True)
    inner = jnp.sum(lifted * mixed, axis=1, keepdims=True)
    lanes = lax.broadcasted_iota(jnp.int32, (tokens, 128), 1)
    both = jnp.where(lanes == 0, power, jnp.where(lanes == 1, inner, 0.0)).T[:2]
    sums_ref[...] = jnp.broadcast_to(both[None], sums_ref.shape)


def token_scales(sums_ref):
    total = jnp.sum(sums_ref[...], axis=0)
    padded = jnp.concatenate([total, jnp.zeros((126, total.shape[1]), F32)], axis=0).T
    scale = lax.rsqrt(padded[:, 0:1] / D + EPSILON)
    return scale, padded[:, 1:2] / D


def grad_kernel(sums_ref, mixed_ref, staged_ref, gain_ref, source_ref, taps_ref, grad_ref):
    scale, inner = token_scales(sums_ref)
    lifted = staged_ref[2].astype(F32) * gain_ref[...].astype(F32)
    mixed_grad = scale * (lifted - mixed_ref[0] * (scale * scale * inner))
    conv_grad = mixed_grad * staged_ref[1].astype(F32)
    grad_ref[...] = conv_grad.T.reshape(grad_ref.shape).astype(BF16)


def token_kernel(sums_ref, mixed_ref, staged_ref, gain_ref, normed_ref, residual_grad_ref, gate_grad_ref):
    scale, inner = token_scales(sums_ref)
    gain = gain_ref[...].astype(F32)
    mixed = mixed_ref[0]
    lifted = staged_ref[2].astype(F32) * gain
    normed_ref[...] = (mixed * scale * gain).astype(BF16)
    mixed_grad = scale * (lifted - mixed * (scale * scale * inner))
    residual_grad_ref[...] = mixed_grad.astype(BF16)
    gate_grad_ref[...] = (mixed_grad * mixed_ref[1]).astype(BF16)


def backward_kernel(spans_ref, slabs_ref, source_ref, taps_ref, table_ref, mixed_ref, out_ref, up_ref, spec_ref, lag_ref):
    signs = half_signs()
    up = to_spectrum(block_rows(slabs_ref[...].astype(F32)), table_ref)
    spec_ref[pl.ds(0, BLOCKS)] = up.reshape(BLOCKS, 8, SPEC)
    up_ref[...] = jnp.zeros((ROWS, 8, SPEC), F32)
    for doc in range(DOCS):
        start, end = doc_bounds(spans_ref, doc)

        @pl.loop(start, end)
        def _(n):
            up_ref[n + PAD * (doc + 1)] = spec_ref[n]

    zero_gaps(spans_ref, spec_ref, 0)
    for doc in range(DOCS):
        start, end = doc_bounds(spans_ref, doc)
        shift = PAD * (doc + 1)

        @pl.loop(0, tiles(end - start))
        def _(tile):
            first = start + TILE * tile

            def step(sums, k, count):
                if count == TILE:
                    return add_group(sums, up_ref, first + TILE + k + shift, taps_ref, TILE + k + LAG_PAD, True)
                rows = [first + TILE + k + shift + j for j in range(count)]
                return add_rows(sums, up_ref, rows, taps_ref, TILE + k + LAG_PAD, True)

            rows = [first + shift + j for j in range(TILE)]
            sums = add_rows(zero_sums(), up_ref, rows, taps_ref, LAG_PAD, True, triangle=True)
            store_tile(spec_ref, first, add_range(sums, end - first - TILE, step))

    lag_ref[...] = jnp.zeros(lag_ref.shape, F32)
    for doc in range(DOCS):
        start, end = doc_bounds(spans_ref, doc)
        begin = start + PAD * (doc + 1)

        @pl.loop(0, tiles(end - start))
        def _(tile):
            first = TILE * tile

            def step(sums, k, count):
                if count == TILE:
                    return add_group(sums, up_ref, begin + first + TILE + k, source_ref, begin + TILE + k, True)
                rows = [begin + first + TILE + k + j for j in range(count)]
                return add_rows(sums, up_ref, rows, source_ref, begin + TILE + k, True)

            rows = [begin + first + j for j in range(TILE)]
            sums = add_rows(load_tile(lag_ref, first), up_ref, rows, source_ref, begin, True, triangle=True)
            store_tile(lag_ref, first, add_range(sums, end - start - first - TILE, step))

    source_grad = from_spectrum(spec_ref[pl.ds(0, BLOCKS)].reshape(BLOCKS * 8, SPEC), table_ref)
    lags, later = lag_ref[pl.ds(0, BLOCKS)], lag_ref[pl.ds(1, BLOCKS)]
    folded = jnp.concatenate(
        [
            lags[..., :FREQS] + signs * later[..., FREQS:],
            lags[..., FREQS:] - signs * later[..., :FREQS],
        ],
        axis=2,
    )
    tap_grad = from_spectrum(folded.reshape(BLOCKS * 8, SPEC), table_ref)
    out_ref[...] = jnp.concatenate(
        [
            sender_slabs(source_grad, 8),
            sender_slabs(tap_grad * TOKENS**-0.5, 8),
        ],
        axis=1,
    ).astype(BF16)


def product_kernel(slabs_ref, values_ref, gate_ref, gate_grad_hbm, values_grad_hbm, filter_grad_hbm, gate_grad_ref, values_grad_ref, filter_grad_ref, sems):
    tokens, width = values_ref.shape
    part = tokens // 2
    leaving = []
    for k in range(2):
        rows = pl.ds(k * part, part)
        slabs = slabs_ref[:, :, rows].astype(F32)
        gated_grad = slabs[:, :8].reshape(width, part).T
        filter_grad_ref[rows] = slabs[:, 8:].reshape(width, part).T
        gate_grad_ref[rows] = (gated_grad * values_ref[rows].astype(F32)).astype(BF16)
        values_grad_ref[rows] = (gated_grad * gate_ref[rows].astype(F32)).astype(BF16)
        for which, (ref, hbm) in enumerate(
            (
                (filter_grad_ref, filter_grad_hbm),
                (gate_grad_ref, gate_grad_hbm),
                (values_grad_ref, values_grad_hbm),
            )
        ):
            leaving.append(pltpu.make_async_copy(ref.at[rows], hbm.at[rows], sems.at[which, k]))
            leaving[-1].start()
    for copy in leaving:
        copy.wait()


def call(kernel, ins, outs, scratch=(), limit=24, cost=4_000_000):
    spaces = {"v": pltpu.VMEM, "h": pltpu.HBM, "s": pltpu.SMEM}
    spec = lambda space: pl.BlockSpec(memory_space=spaces[space])
    return pl.pallas_call(
        kernel,
        out_shape=[
            pltpu.HBM(*shape) if space == "h" else jax.ShapeDtypeStruct(*shape)
            for shape, space in outs
        ],
        in_specs=[spec(space) for space in ins],
        out_specs=[spec(space) for _, space in outs],
        scratch_shapes=list(scratch),
        compiler_params=pltpu.CompilerParams(vmem_limit_bytes=limit * 1024 * 1024),
        cost_estimate=pl.CostEstimate(flops=cost, bytes_accessed=cost, transcendentals=0),
    )


def in_hbm(*arrays):
    return [pltpu.with_memory_space_constraint(array, pltpu.HBM) for array in arrays]


def exchange(array, axis):
    return lax.all_to_all(array, axis, split_axis=0, concat_axis=0, tiled=True)


UPS = ((ROWS, 8, SPEC), F32)
SOURCE = ((2 * ROWS, 8, SPEC), F32)
LAGS = ((2 * LAG_ROWS, 8, SPEC), F32)
SUMS = ((PAD + BLOCKS, 8, SPEC), F32)


def vmem(shape):
    return pltpu.VMEM(*shape)


def run_forward(spans, slabs, table):
    single = ((slabs.shape[0], 8, slabs.shape[2]), BF16)
    return call(
        forward_kernel,
        "svv",
        [(single, "v"), (SOURCE, "v"), (LAGS, "v")],
        [vmem(SUMS)],
    )(spans, slabs, table)


def run_backward(spans, slabs, source, taps, table, mixed):
    pair = ((slabs.shape[0], 16, slabs.shape[2]), BF16)
    return call(
        backward_kernel,
        "svvvvv",
        [(pair, "v")],
        [vmem(UPS), vmem(SUMS), vmem(SUMS)],
    )(spans, slabs, source, taps, table, mixed)[0]


def body(exchange, input_gate, output_gate, values, residual, cotangent, filters, gain, spans):
    tokens, width = input_gate.shape
    table = jnp.asarray(window_table())
    like, wide = ((tokens, width), BF16), ((tokens, width), F32)
    pair, single = ((64, 16, tokens), BF16), ((64, 8, tokens), BF16)
    sums_rows = ((8, 2, tokens), F32)
    dma = pltpu.SemaphoreType.DMA

    (outgoing,) = call(
        gate_kernel,
        "hhh",
        [(pair, "h")],
        [vmem(like), vmem(like), vmem(wide), vmem(pair), dma((3, CHUNKS)), dma((CHUNKS,))],
    )(*in_hbm(values, input_gate, filters))
    incoming = exchange(outgoing, "seq")
    (staged,) = call(stage_kernel, "hhh", [(((3, tokens, width), BF16), "v")], [dma((3,))])(
        *in_hbm(residual, output_gate, cotangent)
    )
    incoming, staged, gain = lax.optimization_barrier((incoming, staged, gain))
    conv, source, taps = run_forward(spans, incoming, table)
    conv = exchange(conv, "seq")
    mixed, sums = call(
        mixed_kernel, "vvvvv", [(((2, tokens, width), F32), "v"), (sums_rows, "v")]
    )(conv, staged, gain, source, taps)
    sums = exchange(sums, "chan")
    (conv_grad,) = call(grad_kernel, "vvvvvv", [(single, "v")])(sums, mixed, staged, gain, source, taps)
    conv_grad = exchange(conv_grad, "seq")
    normed, residual_grad, output_gate_grad = call(token_kernel, "vvvv", [(like, "v")] * 3)(
        sums, mixed, staged, gain
    )
    grads = run_backward(spans, conv_grad, source, taps, table, mixed)
    grads = exchange(grads, "seq")
    input_gate_grad, values_grad, filter_grad = call(
        product_kernel,
        "vvv",
        [(like, "h"), (like, "h"), (wide, "h")],
        [vmem(like), vmem(like), vmem(wide), dma((3, 2))],
    )(grads, values, input_gate)
    return (normed, residual_grad, input_gate_grad, output_gate_grad, values_grad, filter_grad)


def shards(input_gate, output_gate, values, residual, cotangent, filters, norm_gain, doc_spans):
    gain = norm_gain.reshape(1, norm_gain.shape[0])
    spans = doc_spans.reshape(2 * DOCS)
    return body(exchange, input_gate, output_gate, values, residual, cotangent, filters, gain, spans)


def solution(mesh):
    split = P("seq", "chan")
    return jax.shard_map(
        shards,
        mesh=mesh,
        in_specs=(split, split, split, split, split, split, P("chan"), P()),
        out_specs=(split,) * 6,
        check_vma=False,
    )
```
